128 devices in a mesh: gx: 32 (over z_hi, x, y), yz: 4 (over z_lo, core).
Axes of the slice: x: 4, y: 4, z: 4 (z_hi: 2, z_lo: 2; z = z_hi * 2 + z_lo), core: 2. Of those that a mesh axis runs over, the one named last changes fastest.
Arguments:
- positions: float32 [3, 6144], P(None, ('gx', 'yz')), may hold values from -6 to 6
- velocities: float32 [3, 6144], P(None, ('gx', 'yz')), may hold values from -6 to 6
- forces_start: float32 [3, 6144], P(None, ('gx', 'yz')), may hold values from -6 to 6
- species: int32 [6144], P(('gx', 'yz')), may hold values from 0 to 7
- live_atoms: int32 [128], P(('gx', 'yz')), may hold values from 12 to 48, as said below
- send_list: int32 [8, 1536], P(None, ('gx', 'yz')), may hold values from 0 to 47, as said below
- neighbours: int32 [6144, 128], P(('gx', 'yz')), may hold values from 0 to 143, as said below
- neighbour_count: int32 [6144], P(('gx', 'yz')), may hold values from 64 to 128
- radial_weight: bfloat16 [8, 512], replicated, may hold values from -4 to 4
- species_embed: bfloat16 [2, 8, 512], replicated, may hold values from -2 to 2
- env_weight: bfloat16 [1, 512, 64], replicated, may hold values from -0.25 to 0.25
- latent_weight: bfloat16 [1, 576, 512], replicated, may hold values from -0.25 to 0.25
- readout: bfloat16 [512], replicated, may hold values from -0.0625 to 0.0625
Outputs:
- positions_end: float32 [3, 6144], P(None, ('gx', 'yz'))
- velocities_end: float32 [3, 6144], P(None, ('gx', 'yz'))
- forces_end: float32 [3, 6144], P(None, ('gx', 'yz'))
The draws below stay inside these ranges and needn't reach their ends.
Inputs may be any that keep to these rules, and one draw needn't show every extreme that they name: `live_atoms`: atoms in use are the first ones of a domain's slots; some domain uses all 48 in every draw. `send_list`: each row names distinct atoms in use of the sending domain. `neighbours`: each entry names an own atom in use or a ghost slot.
All inputs are finite; a program needn't handle non-finite values.
Results may differ from the reference program's by a relative error of at most 0.038.
Values sent between devices are 32-bit elements; how exact they have to be, the bound alone decides.
A program may use at most 64 MiB of HBM per device.

```python
import math
import jax
import jax.numpy as jnp
import numpy as np
from jax import lax

ATOM_DEV = 48
SLOTS = 128
LATENT = 512
FEATURES = 64
BASIS = 8
SPECIES = 8
LAYERS = 1
CENTRES = 4
GHOSTS = 12
ATOMS = 6144
N_GX = 32
N_YZ = 4


def live_counts(key):
    first_key, second_key, third_key = jax.random.split(key, 3)
    devices = N_GX * N_YZ
    first_draw = jax.random.randint(first_key, (devices,), 0, 9)
    second_draw = jax.random.randint(second_key, (devices,), 0, 9)
    factor = 2 + jnp.minimum(6, first_draw * second_draw // 10)
    counts = factor * ATOM_DEV // 8
    chosen = jax.random.randint(third_key, (), 0, devices)
    return jnp.where(jnp.arange(devices) == chosen, ATOM_DEV, counts).astype(jnp.int32)


def draw_live_atoms(key, part):
    return live_counts(key)


def draw_send_list(key, part):
    live_count = live_counts(key)
    key = jax.random.fold_in(key, 11)
    devices = N_GX * N_YZ
    noise_bits = jax.random.randint(key, (devices, 8, ATOM_DEV), 0, 65536)
    slot_ids = jnp.arange(ATOM_DEV, dtype=jnp.int32)
    scores = noise_bits * ATOM_DEV + slot_ids[None, None, :]
    scores = jnp.where(slot_ids[None, None, :] < live_count[:, None, None], scores, -1 - slot_ids[None, None, :])
    chosen = lax.top_k(scores, GHOSTS)[1]
    return chosen.transpose(1, 0, 2).reshape(8, devices * GHOSTS).astype(jnp.int32)


def draw_neighbours(key, part):
    live_count = live_counts(key)
    key = jax.random.fold_in(key, 12)
    devices = N_GX * N_YZ
    span_top = live_count[:, None, None] + 8 * GHOSTS
    raw_draw = jax.random.randint(key, (devices, ATOM_DEV, SLOTS), 0, span_top)
    picked = jnp.where(raw_draw < live_count[:, None, None], raw_draw, ATOM_DEV + raw_draw - live_count[:, None, None])
    return picked.reshape(devices * ATOM_DEV, SLOTS).astype(jnp.int32)


def draw_neighbour_count(key, part):
    key = jax.random.fold_in(key, 13)
    first_key, second_key = jax.random.split(key)
    devices = N_GX * N_YZ
    counts = SLOTS // 2 + jax.random.randint(first_key, (devices, ATOM_DEV), 0, SLOTS // 2 + 1)
    chosen = jax.random.randint(second_key, (devices, 1), 0, ATOM_DEV)
    counts = jnp.where(jnp.arange(ATOM_DEV)[None, :] == chosen, SLOTS, counts)
    return counts.reshape(devices * ATOM_DEV).astype(jnp.int32)


def draw_radial_weight(key, part):
    key = jax.random.fold_in(key, 14)
    sign_key, size_key = jax.random.split(key)
    sign_part = (2 * jax.random.randint(sign_key, (BASIS, LATENT), 0, 2) - 1).astype(jnp.float32)
    magnitude = jax.random.uniform(size_key, (BASIS, LATENT), jnp.float32, 2.5, 4.0)
    return (sign_part * magnitude).astype(jnp.bfloat16)


def plant(entries, key, least, top_value):
    place = [jax.random.randint(jax.random.fold_in(key, axis), (), 0, length) for axis, length in enumerate(entries.shape)]
    longest = entries.shape.index(max(entries.shape))
    neighbour = place[:longest] + [(place[longest] + 1) % entries.shape[longest]] + place[longest + 1:]
    return entries.at[tuple(place)].set(least).at[tuple(neighbour)].set(top_value)


def shard_levels(stream_key, extent, shards, smallest, top_value):
    level = 1.0
    for axis_at, blocks in shards:
        steps = jax.random.uniform(jax.random.fold_in(jax.random.fold_in(stream_key, 6), axis_at), (blocks,), jnp.float32, smallest / len(shards), top_value / len(shards))
        level = level * jnp.repeat(jnp.exp(steps), extent[axis_at] // blocks).reshape((-1,) + (1,) * (len(extent) - 1 - axis_at))
    return level


def rank_table(count, lean):
    loads = [(1 << 20) // math.isqrt(rank ** lean) + 1 for rank in range(1, count + 1)]
    spread = 1 + sum(loads) // (1 << 30)
    return np.cumsum(np.array([max(1, weight // spread) for weight in loads]))


def ranked(own_key, extent, number_of, skew):
    table = rank_table(number_of, skew)
    lot = jax.random.randint(jax.random.fold_in(own_key, 1), extent, 0, int(table[number_of - 1]))
    rank = jnp.searchsorted(jnp.asarray(table, jnp.int32), lot, side="right")
    return jax.random.permutation(jax.random.fold_in(own_key, 2), number_of)[rank].astype(jnp.int32)


def scatter_about(stream_key, shape, width, bound, shards=(), kind=jnp.bfloat16):
    level = shard_levels(stream_key, shape, shards, -0.22, 0.18) if shards else 1.0
    entries = jax.random.normal(stream_key, shape, jnp.float32) * width * level
    return jnp.minimum(jnp.maximum(entries, -bound), bound).astype(kind)


def setup_inputs(seed: int = 0) -> dict:
    keys = jax.random.split(jax.random.key(seed), 14)
    return {
        "positions": scatter_about(keys[0], (3, ATOMS), 1.5, 6.0, ((1, 128),), jnp.float32),
        "velocities": scatter_about(keys[1], (3, ATOMS), 1.0, 6.0, ((1, 128),), jnp.float32),
        "forces_start": scatter_about(keys[2], (3, ATOMS), 1.0, 6.0, ((1, 128),), jnp.float32),
        "species": plant(ranked(keys[3], (ATOMS,), SPECIES, 2), jax.random.fold_in(keys[3], 3), 0, SPECIES - 1).astype(jnp.int32),
        "live_atoms": draw_live_atoms(jax.random.fold_in(keys[13], 71), 0),
        "send_list": draw_send_list(jax.random.fold_in(keys[13], 71), 0),
        "neighbours": draw_neighbours(jax.random.fold_in(keys[13], 71), 0),
        "neighbour_count": draw_neighbour_count(jax.random.fold_in(keys[13], 71), 0),
        "radial_weight": draw_radial_weight(jax.random.fold_in(keys[13], 71), 0),
        "species_embed": scatter_about(keys[9], (2, SPECIES, LATENT), 0.5, 2.0),
        "env_weight": scatter_about(keys[10], (LAYERS, LATENT, FEATURES), LATENT ** -0.5, 0.25),
        "latent_weight": scatter_about(keys[11], (LAYERS, LATENT + FEATURES, LATENT), (LATENT + FEATURES) ** -0.5, 0.25),
        "readout": scatter_about(keys[12], (LATENT,), (16 * LATENT) ** -0.5, 0.0625),
    }


RADIUS = 6.0
STEP = 0.25
COUPLING = 4.0
MASSES = (1.008, 12.011, 14.007, 15.999, 32.06, 22.99, 35.45, 30.97)
OFFSETS = ((-1, -1), (-1, 0), (-1, 1), (0, -1), (0, 1), (1, -1), (1, 0), (1, 1))

def inverse_mass(species):
    inv_total = jnp.zeros(species.shape, jnp.float32)
    for spec_id in range(len(MASSES)):
        inv_total = inv_total + jnp.where(species == spec_id, jnp.float32(1.0 / MASSES[spec_id]), jnp.float32(0.0))
    return inv_total

def block_energy(centre_pos, neigh_pos, centre_kind, neigh_kind, pair_mask, radial_weight, species_embed, env_weight, latent_weight, readout):
    count_c = centre_pos.shape[1]
    slot_n = neigh_pos.shape[2]
    row_count = count_c * slot_n
    scaled = (neigh_pos - centre_pos[:, :, None]) * (1.0 / RADIUS)
    vectors = scaled.reshape(3, row_count)
    square = lax.optimization_barrier(jnp.sum(vectors * vectors, axis=0))
    envelope = jnp.square(jnp.maximum(1.0 - square, 0.0)) * pair_mask.reshape(row_count)
    basis_n = radial_weight.shape[0]
    basis_mid = (jnp.arange(basis_n, dtype=jnp.float32) + 0.5) / basis_n
    basis_vals = jnp.exp(-2.0 * basis_n * basis_n * jnp.square(square[:, None] - basis_mid[None, :]))
    centre_embed = jnp.dot(centre_kind, species_embed[0], preferred_element_type=jnp.float32)
    feat_width = centre_embed.shape[1]
    preact = jnp.dot(basis_vals.astype(jnp.bfloat16), radial_weight, preferred_element_type=jnp.float32)
    preact = preact + jnp.dot(neigh_kind, species_embed[1], preferred_element_type=jnp.float32)
    preact = (preact.reshape(count_c, slot_n, feat_width) + centre_embed[:, None, :]).reshape(row_count, feat_width)
    hidden = jax.nn.silu(preact)
    norm_scale = slot_n ** (-0.5)
    for layer_id in range(env_weight.shape[0]):
        weights = jnp.dot(hidden.astype(jnp.bfloat16), env_weight[layer_id], preferred_element_type=jnp.float32) * envelope[:, None]
        tensor = vectors[:, :, None] * weights[None, :, :]
        grouped = tensor.reshape(3, count_c, slot_n, weights.shape[1])
        centre_tensor = lax.optimization_barrier(jnp.sum(grouped, axis=2)) * norm_scale
        inner_prod = COUPLING * lax.optimization_barrier(jnp.sum(grouped * centre_tensor[:, :, None, :], axis=0)).reshape(row_count, weights.shape[1])
        joined = jnp.concatenate([hidden, inner_prod], axis=1).astype(jnp.bfloat16)
        hidden = hidden + jax.nn.silu(jnp.dot(joined, latent_weight[layer_id], preferred_element_type=jnp.float32))
    pair_energy = jnp.dot(hidden.astype(jnp.bfloat16), readout, preferred_element_type=jnp.float32)
    return jnp.sum(pair_energy * envelope)

def block_update(forces, block_id, ext_pos, ext_kinds, neighbours, counts, live_count, params):
    first = (block_id * CENTRES).astype(jnp.int32)
    centre_pos = lax.dynamic_slice_in_dim(ext_pos, first, CENTRES, 1)
    neigh_idx = lax.dynamic_slice_in_dim(neighbours, first, CENTRES, 0)
    neigh_pos = ext_pos[:, neigh_idx]
    centre_kind = lax.dynamic_slice_in_dim(ext_kinds, first, CENTRES, 0)
    neigh_kind = ext_kinds[neigh_idx.reshape(-1)]
    block_counts = lax.dynamic_slice_in_dim(counts, first, CENTRES, 0)
    slot_n = neighbours.shape[1]
    alive_rows = first + jnp.arange(CENTRES, dtype=jnp.int32) < live_count
    in_use = (jnp.arange(slot_n, dtype=jnp.int32)[None, :] < block_counts[:, None]) & alive_rows[:, None]
    pair_mask = jnp.where(in_use, jnp.float32(1.0), jnp.float32(0.0))

    def energy_of(centre_arg, neigh_arg):
        return block_energy(centre_arg, neigh_arg, centre_kind, neigh_kind, pair_mask, *params)
    energy, pullback = jax.vjp(energy_of, centre_pos, neigh_pos)
    grad_c, grad_n = pullback(jnp.ones_like(energy))
    current = lax.dynamic_slice_in_dim(forces, first, CENTRES, 1)
    forces = lax.dynamic_update_slice_in_dim(forces, current - grad_c, first, 1)
    return forces.at[:, neigh_idx.reshape(-1)].add(-grad_n.reshape(3, -1))

def domain_forces(ext_pos, ext_kinds, neighbours, counts, live_count, params):

    def one_block(forces, block_id):
        return (block_update(forces, block_id, ext_pos, ext_kinds, neighbours, counts, live_count, params), None)
    blocks = jnp.arange(neighbours.shape[0] // CENTRES, dtype=jnp.int32)
    return lax.scan(one_block, jnp.zeros((3, ext_pos.shape[1]), jnp.float32), blocks)[0]

def evaluate(coords, species, send_list, neighbours, neighbour_count, live_atoms, params):
    dev_n = N_GX * N_YZ
    pos_dev = coords.reshape(3, dev_n, ATOM_DEV).transpose(1, 0, 2)
    spec_dev = species.reshape(dev_n, ATOM_DEV)
    sends = send_list.reshape(8, dev_n, GHOSTS).transpose(1, 0, 2)
    sent_pos = jax.vmap(lambda pos_one, send_one: pos_one[:, send_one])(pos_dev, sends)
    sent_spec = jax.vmap(lambda spec_one, send_one: spec_one[send_one])(spec_dev, sends)
    ghost_pos = []
    ghost_spec = []
    for direction, (step_a, step_b) in enumerate(OFFSETS):
        grid_pos = sent_pos[:, :, direction].reshape(N_GX, N_YZ, 3, GHOSTS)
        ghost_pos.append(jnp.roll(grid_pos, (step_a, step_b), axis=(0, 1)).reshape(dev_n, 3, GHOSTS))
        grid_spec = sent_spec[:, direction].reshape(N_GX, N_YZ, GHOSTS)
        ghost_spec.append(jnp.roll(grid_spec, (step_a, step_b), axis=(0, 1)).reshape(dev_n, GHOSTS))
    ext_pos = jnp.concatenate([pos_dev] + ghost_pos, axis=2)
    ext_spec = jnp.concatenate([spec_dev] + ghost_spec, axis=1)
    ext_kinds = (ext_spec[:, :, None] == jnp.arange(SPECIES, dtype=jnp.int32)[None, None, :]).astype(jnp.bfloat16)
    nb_dev = neighbours.reshape(dev_n, ATOM_DEV, SLOTS)
    cnt_dev = neighbour_count.reshape(dev_n, ATOM_DEV)
    ext_forces = lax.map(lambda items: domain_forces(items[0], items[1], items[2], items[3], items[4], params), (ext_pos, ext_kinds, nb_dev, cnt_dev, live_atoms))
    local = ext_forces[:, :, :ATOM_DEV]
    returned = []
    for direction, (step_a, step_b) in enumerate(OFFSETS):
        start_col = ATOM_DEV + direction * GHOSTS
        grid_force = ext_forces[:, :, start_col:start_col + GHOSTS].reshape(N_GX, N_YZ, 3, GHOSTS)
        returned.append(jnp.roll(grid_force, (-step_a, -step_b), axis=(0, 1)).reshape(dev_n, 3, GHOSTS))
    returned = jnp.stack(returned, axis=2)
    local = jax.vmap(lambda force_one, send_one, back_one: force_one.at[:, send_one.reshape(-1)].add(back_one.reshape(3, -1)))(local, sends, returned)
    return local.transpose(1, 0, 2).reshape(3, dev_n * ATOM_DEV)

def reference(positions, velocities, forces_start, species, live_atoms, send_list, neighbours, neighbour_count, radial_weight, species_embed, env_weight, latent_weight, readout):
    params = (radial_weight, species_embed, env_weight, latent_weight, readout)
    inverse = inverse_mass(species)
    half = velocities + 0.5 * STEP * inverse * forces_start
    moved = positions + STEP * half
    forces_mid = evaluate(moved, species, send_list, neighbours, neighbour_count, live_atoms, params)
    velocities_mid = half + 0.5 * STEP * inverse * forces_mid
    half_two = velocities_mid + 0.5 * STEP * inverse * forces_mid
    positions_end = moved + STEP * half_two
    forces_end = evaluate(positions_end, species, send_list, neighbours, neighbour_count, live_atoms, params)
    velocities_end = half_two + 0.5 * STEP * inverse * forces_end
    return (positions_end, velocities_end, forces_end)
```

```python
import functools

import jax
import jax.numpy as jnp
from jax import lax
from jax.experimental import pallas as pl
from jax.experimental.pallas import tpu as pltpu
from jax.sharding import PartitionSpec as P

F32, BF16, I32 = jnp.float32, jnp.bfloat16, jnp.int32
MESH = pl.DeviceIdType.MESH
NT = (((1,), (1,)), ((), ()))

STEP = 0.25
MASSES = (1.008, 12.011, 14.007, 15.999, 32.06, 22.99, 35.45, 30.97)
ATOMS = 48
SLOTS = 128
GHOSTS = 12
N_YZ = 4
EXT = ATOMS + 8 * GHOSTS
NEAR = ATOMS + 2 * GHOSTS
LATENT = 512
FEATURES = 64
SCALE = 4.0 / SLOTS**0.5
CHAINS = 4


def mm(a, b):
    return jnp.dot(a, b, preferred_element_type=F32)


def lanes_of(shape):
    return lax.broadcasted_iota(I32, shape, len(shape) - 1)


def rows_of(shape):
    return lax.broadcasted_iota(I32, shape, 0)


def gather(table, idx):
    return jnp.take_along_axis(table, jnp.broadcast_to(idx, table.shape), axis=1)


def inverse_mass(species):
    total = jnp.zeros(species.shape, F32)
    for kind, mass in enumerate(MASSES):
        total = total + jnp.where(species == kind, jnp.float32(1.0 / mass), jnp.float32(0.0))
    return total


def partners():
    g, q, n = lax.axis_index("gx"), lax.axis_index("yz"), lax.axis_size("gx")
    slab = [(s, g, lax.rem(q + s, N_YZ)) for s in range(1, N_YZ)]
    up, down = lax.rem(g + 1, n), lax.rem(g + n - 1, n)
    above = [(s, up, lax.rem(q + s, N_YZ)) for s in range(N_YZ)]
    below = [(s, down, lax.rem(q + s, N_YZ)) for s in range(N_YZ)]
    return slab, above, below


def greet():
    slab, above, below = partners()
    barrier = pltpu.get_barrier_semaphore()
    for _, g, q in slab + above + below:
        pl.semaphore_signal(barrier, inc=1, device_id=(g, q), device_id_type=MESH)


def greeted():
    pl.semaphore_wait(pltpu.get_barrier_semaphore(), 3 * N_YZ - 1)


def send(src, dst, sems, at, g, q):
    copy = pltpu.make_async_remote_copy(
        src_ref=src,
        dst_ref=dst,
        send_sem=sems.at[0, at],
        recv_sem=sems.at[1, at],
        device_id=(g, q),
        device_id_type=MESH,
    )
    copy.start()
    return copy


def spread(tiles, near, low, high, sems):
    me = lax.axis_index("yz")
    slab, above, below = partners()
    copies = []
    for s, g, q in slab:
        copies.append(send(tiles(q)[0], near.at[me], sems, s - 1, g, q))
    for s, g, q in above:
        copies.append(send(tiles(q)[1], low.at[me], sems, 3 + s, g, q))
    for s, g, q in below:
        copies.append(send(tiles(q)[1], high.at[me], sems, 7 + s, g, q))
    return copies


def assemble(ext_ref, near, low, high):
    lane = lanes_of((8, 128))
    for d in range(N_YZ):
        up, down = (d + 1) % N_YZ, (d - 1) % N_YZ
        ext_ref[d, :, 0:128] = jnp.where(
            lane < ATOMS, near[d], jnp.where(lane < ATOMS + GHOSTS, near[up], near[down])
        )
        hi = jnp.where(lane < 12, high[up], jnp.where(lane < 24, high[d], high[down]))
        lo = jnp.where(lane < 48, low[up], jnp.where(lane < 60, low[d], low[down]))
        ext_ref[d, :, 128:256] = jnp.where(lane < 36, hi, jnp.where(lane < 72, lo, 0.0))


def fold(f_ref, out0, out1):
    lane = lanes_of((8, 128))
    for d in range(N_YZ):
        up, down = (d + 1) % N_YZ, (d - 1) % N_YZ
        out0[d] = jnp.where(
            lane < ATOMS,
            f_ref[d, :, 0:128],
            jnp.where(lane < ATOMS + GHOSTS, f_ref[down, :, 0:128], f_ref[up, :, 0:128]),
        )
        first = (lane < 12) | ((lane >= 36) & (lane < 48))
        second = (lane < 24) | ((lane >= 48) & (lane < 60))
        out1[d] = jnp.where(
            first,
            f_ref[down, :, 128:256],
            jnp.where(second, f_ref[d, :, 128:256], f_ref[up, :, 128:256]),
        )


def three(x):
    hi = x.astype(BF16)
    rest = x - hi.astype(F32)
    mid = rest.astype(BF16)
    low = rest - mid.astype(F32)
    return jnp.concatenate([hi.astype(F32), mid.astype(F32), low, jnp.zeros_like(x)], axis=0).astype(BF16)


def own_forces(near, low, high, pick_ref):
    lane = lanes_of((8, 128))
    sum0 = (near[0] + near[1]) + (near[2] + near[3])
    lo = (low[0] + low[1]) + (low[2] + low[3])
    hi = (high[0] + high[1]) + (high[2] + high[3])
    sum0 = jnp.where(lane < NEAR, sum0, 0.0)
    sum1 = jnp.where(lane < 36, lo, jnp.where(lane < 72, hi, 0.0))
    atom = rows_of((128, 128))
    pick0 = jnp.where(atom == pick_ref[0:1, :], 1.0, 0.0).astype(BF16)
    pick1 = jnp.where(atom == pick_ref[1:2, :], 1.0, 0.0).astype(BF16)
    parts = lax.dot_general(three(sum0), pick0, NT, preferred_element_type=F32)
    parts = parts + lax.dot_general(three(sum1), pick1, NT, preferred_element_type=F32)
    return (parts[0:8] + parts[8:16]) + parts[16:24]


def payload(source, pick_ref):
    return gather(source, pick_ref[0:1, :]), gather(source, pick_ref[1:2, :])


def first_kernel(
    pos_ref, vel_ref, force_ref, spec_ref, live_ref, send_ref, nb_ref, count_ref,
    radial_ref, embed_ref, env_ref, latent_ref, read_ref,
    ext_ref, nball_ref, half_ref, source_ref, pick_ref, w1_ref, lt_ref, li_ref, bw_ref, ew_ref, rad_ref, rc_ref,
    wide, sends, mine, near, low, high, nbs, sems, nbsems,
):
    greet()
    me = lax.axis_index("yz")
    slab, _, _ = partners()
    lane = lanes_of((8, 128))
    row = rows_of((8, 128))

    wide[...] = jnp.zeros_like(wide)
    wide[0, 0:3, 0:ATOMS] = pos_ref[...]
    wide[1, 0:3, 0:ATOMS] = vel_ref[...]
    wide[2, 0:3, 0:ATOMS] = force_ref[...]
    wide[3, 0:1, 0:ATOMS] = spec_ref[...].astype(F32)
    kinds = jnp.broadcast_to(wide[3, 0:1, :], (8, 128))
    half = wide[1] + 0.5 * STEP * inverse_mass(kinds) * wide[2]
    moved = wide[0] + STEP * half
    live = jnp.broadcast_to(live_ref[...].astype(F32), (8, 128))
    source = jnp.where(row < 3, moved, jnp.where(row == 3, kinds, live))
    half_ref[...] = half
    source_ref[...] = source

    sends[...] = jnp.zeros_like(sends)
    sends[:, 0:GHOSTS] = send_ref[...]
    pick0 = jnp.where(lane < ATOMS, lane, 127)
    pick1 = jnp.full((8, 128), 127, I32)
    for block, tile, at in ((3, 0, 48), (4, 0, 60), (0, 1, 0), (1, 1, 12), (2, 1, 24), (5, 1, 36), (6, 1, 48), (7, 1, 60)):
        names = jnp.broadcast_to(sends[block : block + 1, :], (8, 128))
        names = pltpu.roll(names, at, 1) if at else names
        here = (lane >= at) & (lane < at + GHOSTS)
        if tile == 0:
            pick0 = jnp.where(here, names, pick0)
        else:
            pick1 = jnp.where(here, names, pick1)
    pick_ref[...] = jnp.where(row == 0, pick0, pick1)
    tile0, tile1 = payload(source, pick_ref)
    tile0 = jnp.where(row == 4, live, tile0)
    mine[0] = tile0
    mine[1] = tile1
    near[me] = tile0

    diagonal = rows_of((ATOMS, ATOMS)) == lanes_of((ATOMS, ATOMS))
    counts = jnp.sum(jnp.where(diagonal, count_ref[...].astype(F32), 0.0), axis=1, keepdims=True)
    names = nb_ref[...]
    shape = names.shape
    inner = (names >= 84) & (names < 108)
    outer = (names >= ATOMS) & (names < 84)
    names = jnp.where(inner, names - 36, jnp.where(outer, names + 24, names))
    used = (lanes_of(shape).astype(F32) < counts) & (
        rows_of(shape).astype(F32) < jnp.broadcast_to(live_ref[...].astype(F32), shape)
    )
    nbs[me] = jnp.where(used, names, -1)

    greeted()
    copies = spread(lambda q: (mine.at[0], mine.at[1]), near, low, high, sems)
    for s, g, q in slab:
        copies.append(send(nbs.at[me], nbs.at[me], nbsems, s - 1, g, q))

    prepare(radial_ref, embed_ref, env_ref, latent_ref, read_ref, w1_ref, lt_ref, li_ref, bw_ref, ew_ref, rad_ref, rc_ref)

    for copy in copies:
        copy.wait()
    assemble(ext_ref, near, low, high)
    for d in range(N_YZ):
        nball_ref[d * ATOMS : (d + 1) * ATOMS, :] = nbs[d]


def prepare(radial_ref, embed_ref, env_ref, latent_ref, read_ref, w1_ref, lt_ref, li_ref, bw_ref, ew_ref, rad_ref, rc_ref):
    radial = radial_ref[...].astype(F32)
    reads = read_ref[...].astype(F32)
    stack = jnp.concatenate(
        [radial, embed_ref[1].astype(F32), embed_ref[0].astype(F32), jnp.zeros((104, LATENT), F32)], axis=0
    )
    w1_ref[...] = (stack.T * 0.5).astype(BF16)[:, 0:32]
    env = env_ref[0].astype(F32)
    lt_ref[0:FEATURES, :] = env.T.astype(BF16)
    for at in range(0, LATENT, 128):
        rows = latent_ref[0, at : at + 128, :].astype(F32)
        lt_ref[FEATURES : FEATURES + LATENT, at : at + 128] = (rows.T * 0.5).astype(BF16)
        bw_ref[FEATURES + at : FEATURES + at + 128, :] = (rows * (reads * 0.5)).astype(BF16)
    rows = latent_ref[0, LATENT : LATENT + FEATURES, :].astype(F32)
    li_ref[...] = (rows.T * 0.5).astype(BF16)
    bw_ref[0:FEATURES, :] = (rows * (reads * 0.5)).astype(BF16)
    column = jnp.broadcast_to(reads, (128, LATENT)).T
    ew_ref[:, 0:FEATURES] = env_ref[0]
    ew_ref[:, FEATURES : FEATURES + 16] = jnp.where(lanes_of((LATENT, 16)) == 0, column[:, 0:16], 0.0).astype(BF16)
    rad_ref[0:8, :] = (radial * 0.5).astype(BF16)
    rad_ref[8:16, :] = jnp.zeros((8, LATENT), BF16)
    rc_ref[:, 0:128] = column
    rc_ref[:, 128:256] = column


def collect(f_ref, pick_ref, back0, back1, near, low, high, sems):
    me = lax.axis_index("yz")
    greet()
    fold(f_ref, back0, back1)
    near[me] = back0[me]
    greeted()
    for copy in spread(lambda q: (back0.at[q], back1.at[q]), near, low, high, sems):
        copy.wait()
    return own_forces(near, low, high, pick_ref)


def middle_kernel(
    f_ref, half_ref, source_ref, pick_ref,
    ext_ref, half_two_ref, next_ref, end_ref,
    back0, back1, near, low, high, sems, mine, near2, low2, high2, sems2,
):
    me = lax.axis_index("yz")
    row = rows_of((8, 128))
    forces = collect(f_ref, pick_ref, back0, back1, near, low, high, sems)
    source = source_ref[...]
    kick = 0.5 * STEP * inverse_mass(jnp.broadcast_to(source[3:4], (8, 128))) * forces
    half_two = (half_ref[...] + kick) + kick
    source = jnp.where(row < 3, source + STEP * half_two, source)
    tile0, tile1 = payload(source, pick_ref)
    tile0 = jnp.where(row == 4, jnp.broadcast_to(source[4:5], (8, 128)), tile0)
    mine[0] = tile0
    mine[1] = tile1
    near2[me] = tile0
    copies = spread(lambda q: (mine.at[0], mine.at[1]), near2, low2, high2, sems2)
    half_two_ref[...] = half_two
    next_ref[...] = source
    end_ref[...] = source[0:3, 0:ATOMS]
    for copy in copies:
        copy.wait()
    assemble(ext_ref, near2, low2, high2)


def last_kernel(
    f_ref, half_ref, source_ref, pick_ref,
    vel_ref, force_ref,
    back0, back1, near, low, high, sems,
):
    forces = collect(f_ref, pick_ref, back0, back1, near, low, high, sems)
    kick = 0.5 * STEP * inverse_mass(jnp.broadcast_to(source_ref[3:4, :], (8, 128))) * forces
    vel_ref[...] = (half_ref[...] + kick)[0:3, 0:ATOMS]
    force_ref[...] = forces[0:3, 0:ATOMS]


def chain(items, ext_ref, nb_ref, w1_ref, lt_ref, li_ref, bw_ref, ew_ref, rad_ref, rc_ref, f_ref):
    kind = rows_of((8, 128)).astype(F32)
    mid = (kind + 0.5) * 0.125
    geo, inputs = [], []
    for domain, slot, active in items:
        names = nb_ref[pl.ds(domain * ATOMS + slot, 1), :]
        valid = (names >= 0) & active
        names = jnp.maximum(names, 0)
        here = names < NEAR
        place = jnp.where(here, names, names - NEAR)
        tile0 = ext_ref[domain, :, 0:128]
        neigh = jnp.where(here, gather(tile0, place), gather(ext_ref[domain, :, 128:256], place))
        centre = gather(tile0, jnp.full((1, 128), slot, I32))
        u = (neigh - centre) * (1.0 / 6.0)
        sq = u[0:1] * u[0:1] + u[1:2] * u[1:2] + u[2:3] * u[2:3]
        inside = jnp.where(valid, jnp.maximum(1.0 - sq, 0.0), 0.0)
        env = inside * inside
        delta = sq - mid
        basis = jnp.exp(-128.0 * delta * delta)
        theirs = jnp.where(kind == neigh[3:4], 1.0, 0.0)
        own = jnp.where(kind == centre[3:4], 1.0, 0.0)
        inputs.append(jnp.concatenate([basis, theirs, own, jnp.zeros((8, 128), F32)], axis=0).astype(BF16))
        geo.append((names, u, inside, env, basis * delta))
    hp = mm(w1_ref[...], jnp.concatenate(inputs, axis=1)).astype(BF16)
    yield
    y1 = 1.0 + jnp.tanh(hp)
    h0 = hp * y1
    d1 = y1 + h0 * (2.0 - y1)
    yield
    zv = mm(lt_ref[...], h0)
    yield
    inner, kept = [], []
    for c, (names, u, inside, env, slope) in enumerate(geo):
        z = zv[0:FEATURES, c * 128 : c * 128 + 128]
        ue = [u[k : k + 1] * env for k in range(3)]
        c4 = [jnp.sum(z * ue[k], axis=1, keepdims=True) * SCALE for k in range(3)]
        q = c4[0] * ue[0] + c4[1] * ue[1] + c4[2] * ue[2]
        inner.append((z * q).astype(BF16))
        kept.append((z, ue, c4, q))
    yield
    vp = (zv[FEATURES:] + mm(li_ref[...], jnp.concatenate(inner, axis=1))).astype(BF16)
    yield
    y2 = 1.0 + jnp.tanh(vp)
    s2 = vp * y2
    d2 = y2 + s2 * (2.0 - y2)
    p = jnp.sum((h0 + s2).astype(F32) * rc_ref[...], axis=0, keepdims=True)
    yield
    dj = mm(bw_ref[...], d2)
    yield
    sums, dws = [], []
    for c, (names, u, inside, env, slope) in enumerate(geo):
        z, ue, c4, q = kept[c]
        di = dj[0:FEATURES, c * 128 : c * 128 + 128]
        y = di * z
        g = [jnp.sum(y * (ue[k] * env), axis=1, keepdims=True) * SCALE for k in range(3)]
        dws.append(di * q + g[0] * u[0:1] + g[1] * u[1:2] + g[2] * u[2:3])
        ye = y * env
        sums.append([jnp.sum(c4[k] * ye + g[k] * z, axis=0, keepdims=True) for k in range(3)])
    dw = jnp.concatenate(dws, axis=1)
    ones = jnp.ones((8, dw.shape[1]), F32)
    dw = jnp.concatenate([dw, ones, jnp.zeros_like(ones)], axis=0).astype(BF16)
    yield
    a = dj[FEATURES:] + mm(ew_ref[...], dw)
    yield
    db = mm(rad_ref[...], a.astype(BF16) * d1)
    yield
    for c, (names, u, inside, env, slope) in enumerate(geo):
        domain, slot, active = items[c]
        lanes = slice(c * 128, c * 128 + 128)
        s = sums[c]
        dsq = env * jnp.sum(db[0:8, lanes] * slope, axis=0, keepdims=True) * -256.0
        denv = p[:, lanes] + u[0:1] * s[0] + u[1:2] * s[1] + u[2:3] * s[2]
        twice = 2.0 * (dsq - 2.0 * inside * denv)
        rows = [(env * s[k] + u[k : k + 1] * twice) * (1.0 / 6.0) for k in range(3)]
        du = jnp.concatenate(rows + [jnp.zeros((5, 128), F32)], axis=0)
        hi = du.astype(BF16)
        parts = jnp.concatenate([hi.astype(F32), du - hi.astype(F32)], axis=0).astype(BF16)
        pick = jnp.where(rows_of((EXT, 128)) == names, 1.0, 0.0).astype(BF16)
        out = lax.dot_general(parts, pick, NT, preferred_element_type=F32)
        out = out[0:8] + out[8:16]
        total = jnp.sum(du, axis=1, keepdims=True)
        f_ref[domain] += jnp.where(lanes_of((8, EXT)) == slot, total, 0.0) - out
    yield


def pair_kernel(ext_ref, nb_ref, w1_ref, lt_ref, li_ref, bw_ref, ew_ref, rad_ref, rc_ref, f_ref, sums):
    sums[...] = jnp.zeros_like(sums)
    ends = []
    total = jnp.int32(0)
    for d in range(N_YZ):
        total = total + jnp.max(ext_ref[d, 4:5, 0:1]).astype(I32)
        ends.append(total)
    me = lax.axis_index("yz")
    first = (total * me) // N_YZ
    last = (total * (me + 1)) // N_YZ
    steps = (last - first + 2 * CHAINS - 1) // (2 * CHAINS)

    def step(b, carry):
        chains = []
        for g in range(CHAINS):
            items = []
            for c in range(2):
                at = first + (b * CHAINS + g) * 2 + c
                active = at < last
                at = jnp.minimum(at, total - 1)
                domain = sum((at >= e).astype(I32) for e in ends[:-1])
                base = jnp.where(at >= ends[2], ends[2], jnp.where(at >= ends[1], ends[1], jnp.where(at >= ends[0], ends[0], 0)))
                items.append((domain, at - base, active))
            chains.append(chain(items, ext_ref, nb_ref, w1_ref, lt_ref, li_ref, bw_ref, ew_ref, rad_ref, rc_ref, sums))
        while chains:
            chains = [one for one in chains if next(one, chains) is not chains]
        return carry

    lax.fori_loop(0, steps, step, 0)
    lane = lanes_of((8, 128))
    for d in range(N_YZ):
        tile0 = sums[d, :, 0:128]
        f_ref[d, :, 0:128] = jnp.where(lane < NEAR, tile0, 0.0)
        tail = jnp.concatenate([sums[d, :, 128:EXT], jnp.zeros((8, 256 - EXT), F32)], axis=1)
        far = jnp.where(lane < 128 - NEAR, pltpu.roll(tile0, 128 - NEAR, 1), pltpu.roll(tail, 128 - NEAR, 1))
        f_ref[d, :, 128:256] = jnp.where(lane < NEAR, far, 0.0)


def body(
    positions, velocities, forces_start, species, live_atoms, send_list, neighbours, neighbour_count,
    radial_weight, species_embed, env_weight, latent_weight, readout,
):
    vm = pl.BlockSpec(memory_space=pltpu.VMEM)
    tile = jax.ShapeDtypeStruct((8, 128), F32)
    lists = jax.ShapeDtypeStruct((N_YZ, 8, 256), F32)
    atoms = jax.ShapeDtypeStruct((3, ATOMS), F32)
    four = pltpu.VMEM((N_YZ, 8, 128), F32)
    copies = pltpu.SemaphoreType.DMA((2, 3 * N_YZ - 1))
    params = functools.partial(pltpu.CompilerParams, vmem_limit_bytes=48 << 20)

    args = (
        positions, velocities, forces_start, species.reshape(1, -1), live_atoms.reshape(1, 1), send_list, neighbours,
        neighbour_count.reshape(1, -1), radial_weight, species_embed, env_weight, latent_weight, readout.reshape(1, -1),
    )
    weights = [(LATENT, 32), (FEATURES + LATENT, LATENT), (LATENT, FEATURES), (FEATURES + LATENT, LATENT), (LATENT, FEATURES + 16), (16, LATENT)]
    out_shape = [lists, jax.ShapeDtypeStruct((N_YZ * ATOMS, SLOTS), I32), tile, tile, jax.ShapeDtypeStruct((8, 128), I32)]
    out_shape += [jax.ShapeDtypeStruct(s, BF16) for s in weights] + [jax.ShapeDtypeStruct((LATENT, 256), F32)]
    ext, names, half, source, pick, *prepared = pl.pallas_call(
        first_kernel,
        out_shape=out_shape,
        in_specs=[vm] * len(args),
        out_specs=[vm] * len(out_shape),
        scratch_shapes=[
            pltpu.VMEM((4, 8, 128), F32), pltpu.VMEM((8, 128), I32), pltpu.VMEM((2, 8, 128), F32), four, four, four,
            pltpu.VMEM((N_YZ, ATOMS, SLOTS), I32), copies, pltpu.SemaphoreType.DMA((2, N_YZ - 1)),
        ],
        compiler_params=params(collective_id=0, has_side_effects=True),
    )(*args)

    def forces_of(ext):
        return pl.pallas_call(
            pair_kernel,
            out_shape=lists,
            in_specs=[vm] * 9,
            out_specs=vm,
            scratch_shapes=[pltpu.VMEM((N_YZ, 8, EXT), F32)],
            compiler_params=params(),
        )(ext, names, *prepared)

    returning = [four] * 5 + [copies]
    ext, half, source, positions_end = pl.pallas_call(
        middle_kernel,
        out_shape=[lists, tile, tile, atoms],
        in_specs=[vm] * 4,
        out_specs=[vm] * 4,
        scratch_shapes=returning + [pltpu.VMEM((2, 8, 128), F32), four, four, four, copies],
        compiler_params=params(collective_id=1, has_side_effects=True),
    )(forces_of(ext), half, source, pick)

    velocities_end, forces_end = pl.pallas_call(
        last_kernel,
        out_shape=[atoms, atoms],
        in_specs=[vm] * 4,
        out_specs=[vm] * 2,
        scratch_shapes=returning,
        compiler_params=params(collective_id=2, has_side_effects=True),
    )(forces_of(ext), half, source, pick)
    return positions_end, velocities_end, forces_end


def solution(mesh):
    both = ("gx", "yz")
    atom = P(None, both)
    return jax.shard_map(
        body,
        mesh=mesh,
        in_specs=(atom, atom, atom, P(both), P(both), atom, P(both, None), P(both), P(), P(), P(), P(), P()),
        out_specs=(atom, atom, atom),
        check_vma=False,
    )
```

```python
import functools

import jax
import jax.numpy as jnp
from jax import lax
from jax.experimental import pallas as pl
from jax.experimental.pallas import tpu as pltpu
from jax.sharding import PartitionSpec as P

F32, BF16, I32 = jnp.float32, jnp.bfloat16, jnp.int32
MESH = pl.DeviceIdType.MESH
NT = (((1,), (1,)), ((), ()))

STEP = 0.25
MASSES = (1.008, 12.011, 14.007, 15.999, 32.06, 22.99, 35.45, 30.97)
ATOMS = 48
SLOTS = 128
GHOSTS = 12
N_YZ = 4
EXT = ATOMS + 8 * GHOSTS
NEAR = ATOMS + 2 * GHOSTS
LATENT = 512
FEATURES = 64
SCALE = 4.0 / SLOTS**0.5
CHAINS = 6
SURE = 12


def mm(a, b):
    return jnp.dot(a, b, preferred_element_type=F32)


def lanes_of(shape):
    return lax.broadcasted_iota(I32, shape, len(shape) - 1)


def rows_of(shape):
    return lax.broadcasted_iota(I32, shape, 0)


def gather(table, idx):
    return jnp.take_along_axis(table, jnp.broadcast_to(idx, table.shape), axis=1)


def inverse_mass(species):
    total = jnp.zeros(species.shape, F32)
    for kind, mass in enumerate(MASSES):
        total = total + jnp.where(species == kind, jnp.float32(1.0 / mass), jnp.float32(0.0))
    return total


def partners():
    g, q, n = lax.axis_index("gx"), lax.axis_index("yz"), lax.axis_size("gx")
    slab = [(s, g, lax.rem(q + s, N_YZ)) for s in range(1, N_YZ)]
    up, down = lax.rem(g + 1, n), lax.rem(g + n - 1, n)
    above = [(s, up, lax.rem(q + s, N_YZ)) for s in range(N_YZ)]
    below = [(s, down, lax.rem(q + s, N_YZ)) for s in range(N_YZ)]
    return slab, above, below


def greet():
    slab, above, below = partners()
    barrier = pltpu.get_barrier_semaphore()
    for _, g, q in slab + above + below:
        pl.semaphore_signal(barrier, inc=1, device_id=(g, q), device_id_type=MESH)


def greeted():
    pl.semaphore_wait(pltpu.get_barrier_semaphore(), 3 * N_YZ - 1)


def send(src, dst, sems, at, g, q):
    copy = pltpu.make_async_remote_copy(
        src_ref=src,
        dst_ref=dst,
        send_sem=sems.at[0, at],
        recv_sem=sems.at[1, at],
        device_id=(g, q),
        device_id_type=MESH,
    )
    copy.start()
    return copy


def spread(tiles, near, low, high, sems):
    me = lax.axis_index("yz")
    slab, above, below = partners()
    copies = []
    for s, g, q in slab:
        copies.append(send(tiles(q)[0], near.at[me], sems, s - 1, g, q))
    for s, g, q in above:
        copies.append(send(tiles(q)[1], low.at[me], sems, 3 + s, g, q))
    for s, g, q in below:
        copies.append(send(tiles(q)[1], high.at[me], sems, 7 + s, g, q))
    return copies


def assemble(ext_ref, near, low, high):
    lane = lanes_of((8, 128))
    for d in range(N_YZ):
        up, down = (d + 1) % N_YZ, (d - 1) % N_YZ
        ext_ref[d, :, 0:128] = jnp.where(
            lane < ATOMS, near[d], jnp.where(lane < ATOMS + GHOSTS, near[up], near[down])
        )
        hi = jnp.where(lane < 12, high[up], jnp.where(lane < 24, high[d], high[down]))
        lo = jnp.where(lane < 48, low[up], jnp.where(lane < 60, low[d], low[down]))
        ext_ref[d, :, 128:256] = jnp.where(lane < 36, hi, jnp.where(lane < 72, lo, 0.0))


def fold(f_ref, out0, out1):
    lane = lanes_of((8, 128))
    for d in range(N_YZ):
        up, down = (d + 1) % N_YZ, (d - 1) % N_YZ
        out0[d] = jnp.where(
            lane < ATOMS,
            f_ref[d, :, 0:128],
            jnp.where(lane < ATOMS + GHOSTS, f_ref[down, :, 0:128], f_ref[up, :, 0:128]),
        )
        first = (lane < 12) | ((lane >= 36) & (lane < 48))
        second = (lane < 24) | ((lane >= 48) & (lane < 60))
        out1[d] = jnp.where(
            first,
            f_ref[down, :, 128:256],
            jnp.where(second, f_ref[d, :, 128:256], f_ref[up, :, 128:256]),
        )


def three(x):
    hi = x.astype(BF16)
    rest = x - hi.astype(F32)
    mid = rest.astype(BF16)
    low = rest - mid.astype(F32)
    return jnp.concatenate([hi.astype(F32), mid.astype(F32), low, jnp.zeros_like(x)], axis=0).astype(BF16)


def gathered(near, low, high):
    lane = lanes_of((8, 128))
    sum0 = (near[0] + near[1]) + (near[2] + near[3])
    lo = (low[0] + low[1]) + (low[2] + low[3])
    hi = (high[0] + high[1]) + (high[2] + high[3])
    sum0 = jnp.where(lane < NEAR, sum0, 0.0)
    return sum0, jnp.where(lane < 36, lo, jnp.where(lane < 72, hi, 0.0))


def own_forces(sum0, sum1, pick_ref):
    atom = rows_of((128, 128))
    pick0 = jnp.where(atom == pick_ref[0:1, :], 1.0, 0.0).astype(BF16)
    pick1 = jnp.where(atom == pick_ref[1:2, :], 1.0, 0.0).astype(BF16)
    parts = lax.dot_general(three(sum0), pick0, NT, preferred_element_type=F32)
    parts = parts + lax.dot_general(three(sum1), pick1, NT, preferred_element_type=F32)
    return (parts[0:8] + parts[8:16]) + parts[16:24]


def payload(source, pick_ref):
    return gather(source, pick_ref[0:1, :]), gather(source, pick_ref[1:2, :])


def first_kernel(
    in_refs,
    ext_ref, nball_ref, half_ref, source_ref, pick_ref, w1_ref, lt_ref, li_ref, bw_ref, ew_ref, rad_ref, rc_ref,
    wide, sends, mine, near, low, high, nbs, sems, nbsems, latent, landed,
):
    greet()
    pos_ref, vel_ref, force_ref, spec_ref, live_ref, send_ref, nb_ref, count_ref = in_refs[:8]
    radial_ref, embed_ref, env_ref, latent_ref, read_ref = in_refs[8:]
    load = pltpu.make_async_copy(latent_ref, latent, landed)
    load.start()
    me = lax.axis_index("yz")
    slab, _, _ = partners()
    lane = lanes_of((8, 128))
    row = rows_of((8, 128))

    wide[...] = jnp.zeros_like(wide)
    wide[0, 0:3, 0:ATOMS] = pos_ref[...]
    wide[1, 0:3, 0:ATOMS] = vel_ref[...]
    wide[2, 0:3, 0:ATOMS] = force_ref[...]
    wide[3, 0:1, 0:ATOMS] = spec_ref[...].astype(F32)
    kinds = jnp.broadcast_to(wide[3, 0:1, :], (8, 128))
    half = wide[1] + 0.5 * STEP * inverse_mass(kinds) * wide[2]
    moved = wide[0] + STEP * half
    live = jnp.broadcast_to(live_ref[...].astype(F32), (8, 128))
    source = jnp.where(row < 3, moved, jnp.where(row == 3, kinds, live))
    half_ref[...] = half
    source_ref[...] = source

    sends[...] = jnp.zeros_like(sends)
    sends[:, 0:GHOSTS] = send_ref[...]
    pick0 = jnp.where(lane < ATOMS, lane, 127)
    pick1 = jnp.full((8, 128), 127, I32)
    for block, tile, at in ((3, 0, 48), (4, 0, 60), (0, 1, 0), (1, 1, 12), (2, 1, 24), (5, 1, 36), (6, 1, 48), (7, 1, 60)):
        names = jnp.broadcast_to(sends[block : block + 1, :], (8, 128))
        names = pltpu.roll(names, at, 1) if at else names
        here = (lane >= at) & (lane < at + GHOSTS)
        if tile == 0:
            pick0 = jnp.where(here, names, pick0)
        else:
            pick1 = jnp.where(here, names, pick1)
    pick_ref[...] = jnp.where(row == 0, pick0, pick1)
    tile0, tile1 = payload(source, pick_ref)
    tile0 = jnp.where(row == 4, live, tile0)
    mine[0] = tile0
    mine[1] = tile1
    near[me] = tile0

    diagonal = rows_of((ATOMS, ATOMS)) == lanes_of((ATOMS, ATOMS))
    counts = jnp.sum(jnp.where(diagonal, count_ref[...].astype(F32), 0.0), axis=1, keepdims=True)
    names = nb_ref[...]
    shape = names.shape
    inner = (names >= 84) & (names < 108)
    outer = (names >= ATOMS) & (names < 84)
    names = jnp.where(inner, names - 36, jnp.where(outer, names + 24, names))
    used = (lanes_of(shape).astype(F32) < counts) & (
        rows_of(shape).astype(F32) < jnp.broadcast_to(live_ref[...].astype(F32), shape)
    )
    nbs[me] = jnp.where(used, names, -1)

    greeted()
    copies = spread(lambda q: (mine.at[0], mine.at[1]), near, low, high, sems)
    for s, g, q in slab:
        copies.append(send(nbs.at[me], nbs.at[me], nbsems, s - 1, g, q))

    load.wait()
    prepare(radial_ref, embed_ref, env_ref, latent, read_ref, w1_ref, lt_ref, li_ref, bw_ref, ew_ref, rad_ref, rc_ref)

    for copy in copies:
        copy.wait()
    assemble(ext_ref, near, low, high)
    for d in range(N_YZ):
        nball_ref[d * ATOMS : (d + 1) * ATOMS, :] = nbs[d]


def prepare(radial_ref, embed_ref, env_ref, latent_ref, read_ref, w1_ref, lt_ref, li_ref, bw_ref, ew_ref, rad_ref, rc_ref):
    radial = radial_ref[...].astype(F32)
    reads = read_ref[...].astype(F32).reshape(1, LATENT)
    stack = jnp.concatenate(
        [radial, embed_ref[1].astype(F32), embed_ref[0].astype(F32), jnp.zeros((104, LATENT), F32)], axis=0
    )
    w1_ref[...] = (stack.T * 0.5).astype(BF16)[:, 0:32]
    lt_ref[0:FEATURES, :] = env_ref[0].astype(F32).T.astype(BF16)
    for at in range(0, LATENT, 128):
        rows = latent_ref[0, at : at + 128, :].astype(F32)
        lt_ref[FEATURES : FEATURES + LATENT, at : at + 128] = (rows.T * 0.5).astype(BF16)
        bw_ref[FEATURES + at : FEATURES + at + 128, :] = (rows * (reads * 0.5)).astype(BF16)
    rows = latent_ref[0, LATENT : LATENT + FEATURES, :].astype(F32)
    li_ref[...] = (rows.T * 0.5).astype(BF16)
    bw_ref[0:FEATURES, :] = (rows * (reads * 0.5)).astype(BF16)
    column = jnp.broadcast_to(reads, (128, LATENT)).T
    ew_ref[:, 0:FEATURES] = env_ref[0]
    ew_ref[:, FEATURES : FEATURES + 16] = jnp.where(lanes_of((LATENT, 16)) == 0, column[:, 0:16], 0.0).astype(BF16)
    rad_ref[0:8, :] = (radial * 0.5).astype(BF16)
    rad_ref[8:16, :] = jnp.zeros((8, LATENT), BF16)
    rc_ref[...] = column


def collect(f_ref, refs, fsum, own, back0, back1, near, low, high, sems):
    me = lax.axis_index("yz")
    greet()
    sure_forces(fsum, own, f_ref, refs)
    fold(fsum, back0, back1)
    near[me] = back0[me]
    greeted()
    for copy in spread(lambda q: (back0.at[q], back1.at[q]), near, low, high, sems):
        copy.wait()
    return gathered(near, low, high)


def middle_kernel(
    f_ref, half_ref, source_ref, pick_ref, *rest
):
    refs, (next_ext_ref, half_two_ref, next_ref), scratch = rest[:9], rest[9:12], rest[12:]
    mine, near, low, high, sems = scratch[8:]
    me = lax.axis_index("yz")
    row = rows_of((8, 128))
    forces = own_forces(*collect(f_ref, refs, *scratch[:8]), pick_ref)
    source = source_ref[...]
    kick = 0.5 * STEP * inverse_mass(jnp.broadcast_to(source[3:4], (8, 128))) * forces
    half_two = (half_ref[...] + kick) + kick
    source = jnp.where(row < 3, source + STEP * half_two, source)
    tile0, tile1 = payload(source, pick_ref)
    tile0 = jnp.where(row == 4, jnp.broadcast_to(source[4:5], (8, 128)), tile0)
    mine[0] = tile0
    mine[1] = tile1
    near[me] = tile0
    copies = spread(lambda q: (mine.at[0], mine.at[1]), near, low, high, sems)
    half_two_ref[...] = half_two
    next_ref[...] = source
    for copy in copies:
        copy.wait()
    assemble(next_ext_ref, near, low, high)


def last_kernel(f_ref, *rest):
    refs, total_ref, scratch = rest[:9], rest[9], rest[10:]
    total_ref[0], total_ref[1] = collect(f_ref, refs, *scratch)


def end_kernel(total_ref, half_ref, source_ref, pick_ref, pos_ref, vel_ref, force_ref):
    forces = own_forces(total_ref[0], total_ref[1], pick_ref)
    kick = 0.5 * STEP * inverse_mass(jnp.broadcast_to(source_ref[3:4, :], (8, 128))) * forces
    pos_ref[...] = source_ref[0:3, 0:ATOMS]
    vel_ref[...] = (half_ref[...] + kick)[0:3, 0:ATOMS]
    force_ref[...] = forces[0:3, 0:ATOMS]


def chain(items, add, ext_ref, nb_ref, w1_ref, lt_ref, li_ref, bw_ref, ew_ref, rad_ref, rc_ref):
    kind = rows_of((8, 128)).astype(F32)
    mid = (kind + 0.5) * 0.125
    geo, inputs = [], []
    for domain, slot, active in items:
        names = nb_ref[pl.ds(domain * ATOMS + slot, 1), :]
        valid = (names >= 0) & active
        names = jnp.maximum(names, 0)
        here = names < NEAR
        place = jnp.where(here, names, names - NEAR)
        tile0 = ext_ref[domain, :, 0:128]
        neigh = jnp.where(here, gather(tile0, place), gather(ext_ref[domain, :, 128:256], place))
        centre = gather(tile0, jnp.full((1, 128), slot, I32))
        u = (neigh - centre) * (1.0 / 6.0)
        sq = u[0:1] * u[0:1] + u[1:2] * u[1:2] + u[2:3] * u[2:3]
        inside = jnp.where(valid, jnp.maximum(1.0 - sq, 0.0), 0.0)
        env = inside * inside
        delta = sq - mid
        basis = jnp.exp(-128.0 * delta * delta)
        theirs = jnp.where(kind == neigh[3:4], 1.0, 0.0)
        own = jnp.where(kind == centre[3:4], 1.0, 0.0)
        inputs.append(jnp.concatenate([basis, theirs, own, jnp.zeros((8, 128), F32)], axis=0).astype(BF16))
        geo.append((names, u, inside, env, basis * delta))
    hp = mm(w1_ref[...], jnp.concatenate(inputs, axis=1)).astype(BF16)
    yield
    y1 = 1.0 + jnp.tanh(hp)
    h0 = hp * y1
    d1 = y1 + h0 * (2.0 - y1)
    yield
    zv = mm(lt_ref[...], h0)
    yield
    inner, kept = [], []
    for c, (names, u, inside, env, slope) in enumerate(geo):
        z = zv[0:FEATURES, c * 128 : c * 128 + 128]
        ue = [u[k : k + 1] * env for k in range(3)]
        c4 = [jnp.sum(z * ue[k], axis=1, keepdims=True) * SCALE for k in range(3)]
        q = c4[0] * ue[0] + c4[1] * ue[1] + c4[2] * ue[2]
        inner.append((z * q).astype(BF16))
        kept.append((z, ue, c4, q))
    yield
    vp = (zv[FEATURES:] + mm(li_ref[...], jnp.concatenate(inner, axis=1))).astype(BF16)
    yield
    y2 = 1.0 + jnp.tanh(vp)
    s2 = vp * y2
    d2 = y2 + s2 * (2.0 - y2)
    h2 = (h0 + s2).astype(F32)
    p = [jnp.sum(h2[:, c * 128 : c * 128 + 128] * rc_ref[...], axis=0, keepdims=True) for c in range(len(geo))]
    yield
    dj = mm(bw_ref[...], d2)
    yield
    sums, dws = [], []
    for c, (names, u, inside, env, slope) in enumerate(geo):
        z, ue, c4, q = kept[c]
        di = dj[0:FEATURES, c * 128 : c * 128 + 128]
        y = di * z
        g = [jnp.sum(y * (ue[k] * env), axis=1, keepdims=True) * SCALE for k in range(3)]
        dws.append(di * q + g[0] * u[0:1] + g[1] * u[1:2] + g[2] * u[2:3])
        ye = y * env
        sums.append([jnp.sum(c4[k] * ye + g[k] * z, axis=0, keepdims=True) for k in range(3)])
    dw = jnp.concatenate(dws, axis=1)
    ones = jnp.ones((8, dw.shape[1]), F32)
    dw = jnp.concatenate([dw, ones, jnp.zeros_like(ones)], axis=0).astype(BF16)
    yield
    a = dj[FEATURES:] + mm(ew_ref[...], dw)
    yield
    db = mm(rad_ref[...], a.astype(BF16) * d1)
    yield
    for c, (names, u, inside, env, slope) in enumerate(geo):
        domain, slot, active = items[c]
        lanes = slice(c * 128, c * 128 + 128)
        s = sums[c]
        dsq = env * jnp.sum(db[0:8, lanes] * slope, axis=0, keepdims=True) * -256.0
        denv = p[c] + u[0:1] * s[0] + u[1:2] * s[1] + u[2:3] * s[2]
        twice = 2.0 * (dsq - 2.0 * inside * denv)
        rows = [(env * s[k] + u[k : k + 1] * twice) * (1.0 / 6.0) for k in range(3)]
        du = jnp.concatenate(rows + [jnp.zeros((5, 128), F32)], axis=0)
        hi = du.astype(BF16)
        parts = jnp.concatenate([hi.astype(F32), du - hi.astype(F32)], axis=0).astype(BF16)
        pick = jnp.where(rows_of((EXT, 128)) == names, 1.0, 0.0).astype(BF16)
        out = lax.dot_general(parts, pick, NT, preferred_element_type=F32)
        out = out[0:8] + out[8:16]
        total = jnp.sum(du, axis=1, keepdims=True)
        add(domain, jnp.where(lanes_of((8, EXT)) == slot, total, 0.0) - out)
    yield


def drive(chains):
    while chains:
        chains = [one for one in chains if next(one, chains) is not chains]


def split(tile0, tail):
    lane = lanes_of((8, 128))
    far = jnp.where(lane < 128 - NEAR, pltpu.roll(tile0, 128 - NEAR, 1), pltpu.roll(tail, 128 - NEAR, 1))
    return jnp.where(lane < NEAR, tile0, 0.0), jnp.where(lane < NEAR, far, 0.0)


def pair_kernel(ext_ref, nb_ref, w1_ref, lt_ref, li_ref, bw_ref, ew_ref, rad_ref, rc_ref, f_ref, sums):
    refs = (ext_ref, nb_ref, w1_ref, lt_ref, li_ref, bw_ref, ew_ref, rad_ref, rc_ref)
    sums[...] = jnp.zeros_like(sums)
    ends = []
    total = jnp.int32(0)
    for d in range(N_YZ):
        total = total + jnp.max(ext_ref[d, 4:5, 0:1]).astype(I32) - SURE
        ends.append(total)
    me = lax.axis_index("yz")
    first = (total * me) // N_YZ
    last = (total * (me + 1)) // N_YZ
    steps = lax.max(last - first + CHAINS - 1, 0) // (2 * CHAINS)

    def add(domain, value):
        sums[domain, :, 0:EXT] += value

    def work(start, chains):
        made = []
        for g in range(chains):
            items = []
            for c in range(2):
                at = start + 2 * g + c
                active = at < last
                at = jnp.minimum(at, total - 1)
                domain = sum((at >= e).astype(I32) for e in ends[:-1])
                base = jnp.where(at >= ends[0], ends[0], 0)
                for e in ends[1:-1]:
                    base = jnp.where(at >= e, e, base)
                items.append((domain, at - base + SURE, active))
            made.append(chain(items, add, *refs))
        drive(made)

    def step(b, carry):
        work(first + b * 2 * CHAINS, CHAINS)
        return carry

    lax.fori_loop(0, steps, step, 0)
    rest = first + steps * 2 * CHAINS

    @pl.when(rest < last)
    def _():
        work(rest, CHAINS // 2)

    for d in range(N_YZ):
        f_ref[d, :, 0:128], f_ref[d, :, 128:256] = split(sums[d, :, 0:128], sums[d, :, 128:256])


def sure_forces(fsum, own, f_ref, refs):
    me = lax.axis_index("yz")
    values = []
    chains = []
    for g in range(SURE // 2):
        items = [(me, 2 * g + c, True) for c in range(2)]
        chains.append(chain(items, lambda domain, value: values.append(value), *refs))
    drive(chains)
    own[...] = jnp.zeros_like(own)
    own[:, 0:EXT] = functools.reduce(jnp.add, values)
    fsum[...] = f_ref[...]
    tile0, tile1 = split(own[:, 0:128], own[:, 128:256])
    fsum[me, :, 0:128] += tile0
    fsum[me, :, 128:256] += tile1


def body(
    positions, velocities, forces_start, species, live_atoms, send_list, neighbours, neighbour_count,
    radial_weight, species_embed, env_weight, latent_weight, readout,
):
    vm = pl.BlockSpec(memory_space=pltpu.VMEM)
    tile = jax.ShapeDtypeStruct((8, 128), F32)
    lists = jax.ShapeDtypeStruct((N_YZ, 8, 256), F32)
    atoms = jax.ShapeDtypeStruct((3, ATOMS), F32)
    four = pltpu.VMEM((N_YZ, 8, 128), F32)
    sums = pltpu.VMEM((N_YZ, 8, 256), F32)
    copies = pltpu.SemaphoreType.DMA((2, 3 * N_YZ - 1))
    params = functools.partial(pltpu.CompilerParams, vmem_limit_bytes=48 << 20)

    args = (
        positions, velocities, forces_start, species.reshape(1, -1), live_atoms.reshape(1, 1), send_list, neighbours,
        neighbour_count.reshape(1, -1), radial_weight, species_embed, env_weight, latent_weight,
        readout,
    )
    weights = [(LATENT, 32), (FEATURES + LATENT, LATENT), (LATENT, FEATURES), (FEATURES + LATENT, LATENT), (LATENT, FEATURES + 16), (16, LATENT)]
    out_shape = [lists, jax.ShapeDtypeStruct((N_YZ * ATOMS, SLOTS), I32), tile, tile, jax.ShapeDtypeStruct((8, 128), I32)]
    out_shape += [jax.ShapeDtypeStruct(s, BF16) for s in weights] + [jax.ShapeDtypeStruct((LATENT, 128), F32)]
    scratch = [
        pltpu.VMEM((4, 8, 128), F32), pltpu.VMEM((8, 128), I32), pltpu.VMEM((2, 8, 128), F32), four, four, four,
        pltpu.VMEM((N_YZ, ATOMS, SLOTS), I32), copies, pltpu.SemaphoreType.DMA((2, N_YZ - 1)),
        pltpu.VMEM(latent_weight.shape, BF16), pltpu.SemaphoreType.DMA,
    ]

    def first(*refs):
        first_kernel(refs[: len(args)], *refs[len(args) :])

    ext, names, half, source, pick, *prepared = pl.pallas_call(
        first,
        out_shape=out_shape,
        in_specs=[vm] * 11 + [pl.BlockSpec(memory_space=pl.ANY), vm],
        out_specs=[vm] * len(out_shape),
        scratch_shapes=scratch,
        compiler_params=pltpu.CompilerParams(vmem_limit_bytes=103 << 19, collective_id=0, has_side_effects=True),
    )(*args)

    def forces_of(ext):
        return pl.pallas_call(
            pair_kernel,
            out_shape=lists,
            in_specs=[vm] * 9,
            out_specs=vm,
            scratch_shapes=[sums],
            compiler_params=params(),
        )(ext, names, *prepared)

    returning = [sums, pltpu.VMEM((8, 256), F32)] + [four] * 5 + [copies]
    next_ext, half, source = pl.pallas_call(
        middle_kernel,
        out_shape=[lists, tile, tile],
        in_specs=[vm] * 13,
        out_specs=[vm] * 3,
        scratch_shapes=returning + [pltpu.VMEM((2, 8, 128), F32), four, four, four, copies],
        compiler_params=params(collective_id=1, has_side_effects=True),
    )(forces_of(ext), half, source, pick, ext, names, *prepared)

    totals = pl.pallas_call(
        last_kernel,
        out_shape=jax.ShapeDtypeStruct((2, 8, 128), F32),
        in_specs=[vm] * 10,
        out_specs=vm,
        scratch_shapes=returning,
        compiler_params=params(collective_id=2, has_side_effects=True),
    )(forces_of(next_ext), next_ext, names, *prepared)

    return pl.pallas_call(
        end_kernel,
        out_shape=[atoms] * 3,
        in_specs=[vm] * 4,
        out_specs=[vm] * 3,
        compiler_params=params(),
    )(totals, half, source, pick)


def solution(mesh):
    both = ("gx", "yz")
    atom = P(None, both)
    return jax.shard_map(
        body,
        mesh=mesh,
        in_specs=(atom, atom, atom, P(both), P(both), atom, P(both, None), P(both), P(), P(), P(), P(), P()),
        out_specs=(atom, atom, atom),
        check_vma=False,
    )
```

```python
import functools

import jax
import jax.numpy as jnp
from jax import lax
from jax.experimental import pallas as pl
from jax.experimental.pallas import tpu as pltpu
from jax.sharding import PartitionSpec as P

F32, BF16, I32 = jnp.float32, jnp.bfloat16, jnp.int32
MESH = pl.DeviceIdType.MESH
NT = (((1,), (1,)), ((), ()))

STEP = 0.25
MASSES = (1.008, 12.011, 14.007, 15.999, 32.06, 22.99, 35.45, 30.97)
ATOMS = 48
SLOTS = 128
GHOSTS = 12
N_YZ = 4
EXT = ATOMS + 8 * GHOSTS
NEAR = ATOMS + 2 * GHOSTS
LATENT = 512
FEATURES = 64
SCALE = 4.0 / SLOTS**0.5
CHAINS = 8
LAST = 3
SURE = 14


def mm(a, b):
    return jnp.dot(a, b, preferred_element_type=F32)


def lanes_of(shape):
    return lax.broadcasted_iota(I32, shape, len(shape) - 1)


def rows_of(shape):
    return lax.broadcasted_iota(I32, shape, 0)


def gather(table, idx):
    return jnp.take_along_axis(table, jnp.broadcast_to(idx, table.shape), axis=1)


def inverse_mass(species):
    total = jnp.zeros(species.shape, F32)
    for kind, mass in enumerate(MASSES):
        total = total + jnp.where(species == kind, jnp.float32(1.0 / mass), jnp.float32(0.0))
    return total


def partners():
    g, q, n = lax.axis_index("gx"), lax.axis_index("yz"), lax.axis_size("gx")
    slab = [(s, g, lax.rem(q + s, N_YZ)) for s in range(1, N_YZ)]
    up, down = lax.rem(g + 1, n), lax.rem(g + n - 1, n)
    above = [(s, up, lax.rem(q + s, N_YZ)) for s in range(N_YZ)]
    below = [(s, down, lax.rem(q + s, N_YZ)) for s in range(N_YZ)]
    return slab, above, below


def greet():
    slab, above, below = partners()
    barrier = pltpu.get_barrier_semaphore()
    for _, g, q in slab + above + below:
        pl.semaphore_signal(barrier, inc=1, device_id=(g, q), device_id_type=MESH)


def greeted():
    pl.semaphore_wait(pltpu.get_barrier_semaphore(), 3 * N_YZ - 1)


def wide_partners():
    g, q, n = lax.axis_index("gx"), lax.axis_index("yz"), lax.axis_size("gx")
    column = [lax.rem(q + s, N_YZ) for s in range(N_YZ)]
    return [[(s, lax.rem(g + n + step, n), column[s]) for s in range(step == 0, N_YZ)] for step in (0, 1, -1, 2, -2)]


def send(src, dst, sems, at, g, q):
    copy = pltpu.make_async_remote_copy(
        src_ref=src,
        dst_ref=dst,
        send_sem=sems.at[0, at],
        recv_sem=sems.at[1, at],
        device_id=(g, q),
        device_id_type=MESH,
    )
    copy.start()
    return copy


def spread(tiles, near, low, high, sems):
    me = lax.axis_index("yz")
    slab, above, below = partners()
    copies = []
    for s, g, q in slab:
        copies.append(send(tiles(q)[0], near.at[me], sems, s - 1, g, q))
    for s, g, q in above:
        copies.append(send(tiles(q)[1], low.at[me], sems, 3 + s, g, q))
    for s, g, q in below:
        copies.append(send(tiles(q)[1], high.at[me], sems, 7 + s, g, q))
    return copies


def assemble(ext_ref, near, low, high):
    lane = lanes_of((8, 128))
    for d in range(N_YZ):
        up, down = (d + 1) % N_YZ, (d - 1) % N_YZ
        ext_ref[d, :, 0:128] = jnp.where(
            lane < ATOMS, near[d], jnp.where(lane < ATOMS + GHOSTS, near[up], near[down])
        )
        hi = jnp.where(lane < 12, high[up], jnp.where(lane < 24, high[d], high[down]))
        lo = jnp.where(lane < 48, low[up], jnp.where(lane < 60, low[d], low[down]))
        ext_ref[d, :, 128:256] = jnp.where(lane < 36, hi, jnp.where(lane < 72, lo, 0.0))


def fold(f_ref):
    lane = lanes_of((8, 128))
    first = (lane < 12) | ((lane >= 36) & (lane < 48))
    second = (lane < 24) | ((lane >= 48) & (lane < 60))
    tiles = []
    for d in range(N_YZ):
        up, down = (d + 1) % N_YZ, (d - 1) % N_YZ
        tile0 = jnp.where(
            lane < ATOMS,
            f_ref[d, :, 0:128],
            jnp.where(lane < ATOMS + GHOSTS, f_ref[down, :, 0:128], f_ref[up, :, 0:128]),
        )
        tile1 = jnp.where(
            first,
            f_ref[down, :, 128:256],
            jnp.where(second, f_ref[d, :, 128:256], f_ref[up, :, 128:256]),
        )
        tiles.append((tile0, tile1))
    return tiles


def pack(tiles):
    low = jnp.where(lanes_of((8, 128)) < 64, tiles[0], pltpu.roll(tiles[1], 64, 1))
    high = jnp.where(lanes_of((8, 128)) < 64, tiles[2], pltpu.roll(tiles[3], 64, 1))
    return jnp.where(rows_of((8, 128)) < 4, low, pltpu.roll(high, 4, 0))


def unpack(tile, d):
    tile = pltpu.roll(tile, 64, 1) if d % 2 else tile
    return pltpu.roll(tile, 4, 0) if d >= 2 else tile


def dense(tile, picks):
    hi = tile.astype(BF16)
    parts = jnp.concatenate([hi.astype(F32), tile - hi.astype(F32)], axis=0).astype(BF16)
    hot = jnp.where(rows_of((64, 128)) == picks.astype(I32), 1.0, 0.0).astype(BF16)
    out = lax.dot_general(parts, hot, NT, preferred_element_type=F32)
    return out[0:8] + out[8:16]


def three(x):
    hi = x.astype(BF16)
    rest = x - hi.astype(F32)
    mid = rest.astype(BF16)
    low = rest - mid.astype(F32)
    return jnp.concatenate([hi.astype(F32), mid.astype(F32), low, jnp.zeros_like(x)], axis=0).astype(BF16)


def gathered(near, low, high):
    lane = lanes_of((8, 128))
    sum0 = (near[0] + near[1]) + (near[2] + near[3])
    lo = (low[0] + low[1]) + (low[2] + low[3])
    hi = (high[0] + high[1]) + (high[2] + high[3])
    sum0 = jnp.where(lane < NEAR, sum0, 0.0)
    return sum0, jnp.where(lane < 36, lo, jnp.where(lane < 72, hi, 0.0))


def own_forces(sum0, sum1, pick_ref):
    atom = rows_of((128, 128))
    pick0 = jnp.where(atom == pick_ref[0:1, :], 1.0, 0.0).astype(BF16)
    pick1 = jnp.where(atom == pick_ref[1:2, :], 1.0, 0.0).astype(BF16)
    parts = lax.dot_general(three(sum0), pick0, NT, preferred_element_type=F32)
    parts = parts + lax.dot_general(three(sum1), pick1, NT, preferred_element_type=F32)
    return (parts[0:8] + parts[8:16]) + parts[16:24]


def lists_from(ext_ref, near, near_picks, low, low_picks, high, high_picks):
    assemble(
        ext_ref,
        [gather(near[d], near_picks[d][4:5].astype(I32)) for d in range(N_YZ)],
        [gather(low[d], low_picks[d][5:6].astype(I32)) for d in range(N_YZ)],
        [gather(high[d], high_picks[d][5:6].astype(I32)) for d in range(N_YZ)],
    )


def first_kernel(
    in_refs,
    ext_ref, nball_ref, state_ref, picks_ref, pick_ref, w1_ref, lt_ref, li_ref, bw_ref, ew_ref, rad_ref, rc_ref,
    wide, sends, mine, near, low, high, nbs, sems, nbsems, latent, landed,
):
    greet()
    pos_ref, vel_ref, force_ref, spec_ref, live_ref, send_ref, nb_ref, count_ref = in_refs[:8]
    radial_ref, embed_ref, env_ref, latent_ref, read_ref = in_refs[8:]
    load = pltpu.make_async_copy(latent_ref, latent, landed)
    load.start()
    me = lax.axis_index("yz")
    slab, _, _ = partners()
    lane = lanes_of((8, 128))
    row = rows_of((8, 128))

    wide[...] = jnp.zeros_like(wide)
    wide[0, 0:3, 0:ATOMS] = pos_ref[...]
    wide[1, 0:3, 0:ATOMS] = vel_ref[...]
    wide[2, 0:3, 0:ATOMS] = force_ref[...]
    wide[3, 0:1, 0:ATOMS] = spec_ref[...].astype(F32)
    kinds = jnp.broadcast_to(wide[3, 0:1, :], (8, 128))
    half = wide[1] + 0.5 * STEP * inverse_mass(kinds) * wide[2]
    moved = wide[0] + STEP * half
    live = jnp.broadcast_to(live_ref[...].astype(F32), (8, 128))
    source = jnp.where(row < 3, moved, jnp.where(row == 3, kinds, live))

    sends[...] = jnp.zeros_like(sends)
    sends[:, 0:GHOSTS] = send_ref[...]
    pick0 = jnp.where(lane < ATOMS, lane, 127)
    pick1 = jnp.full((8, 128), 127, I32)
    for block, tile, at in ((3, 0, 48), (4, 0, 60), (0, 1, 0), (1, 1, 12), (2, 1, 24), (5, 1, 36), (6, 1, 48), (7, 1, 60)):
        names = jnp.broadcast_to(sends[block : block + 1, :], (8, 128))
        names = pltpu.roll(names, at, 1) if at else names
        here = (lane >= at) & (lane < at + GHOSTS)
        if tile == 0:
            pick0 = jnp.where(here, names, pick0)
        else:
            pick1 = jnp.where(here, names, pick1)
    pick_ref[...] = jnp.where(row == 0, pick0, pick1)
    mine[0] = source
    mine[1] = jnp.where(row < 3, half, jnp.where(row == 4, pick0.astype(F32), jnp.where(row == 5, pick1.astype(F32), live)))
    near[me] = mine[...]

    diagonal = rows_of((ATOMS, ATOMS)) == lanes_of((ATOMS, ATOMS))
    counts = jnp.sum(jnp.where(diagonal, count_ref[...].astype(F32), 0.0), axis=1, keepdims=True)
    names = nb_ref[...]
    shape = names.shape
    inner = (names >= 84) & (names < 108)
    outer = (names >= ATOMS) & (names < 84)
    names = jnp.where(inner, names - 36, jnp.where(outer, names + 24, names))
    used = (lanes_of(shape).astype(F32) < counts) & (
        rows_of(shape).astype(F32) < jnp.broadcast_to(live_ref[...].astype(F32), shape)
    )
    nbs[me] = jnp.where(used, names, -1)

    greeted()
    copies = spread(lambda q: (mine, mine), near, low, high, sems)
    names = [send(nbs.at[me], nbs.at[me], nbsems, s - 1, g, q) for s, g, q in slab]

    load.wait()
    prepare(radial_ref, embed_ref, env_ref, latent, read_ref, w1_ref, lt_ref, li_ref, bw_ref, ew_ref, rad_ref, rc_ref)

    for copy in copies:
        copy.wait()
    slabs = [[(buffer[d, 0], buffer[d, 1]) for d in range(N_YZ)] for buffer in (low, near, high)]
    places = [[one[0] for one in slab] for slab in slabs]
    others = [[one[1] for one in slab] for slab in slabs]
    lists_from(ext_ref, places[1], others[1], places[0], others[0], places[2], others[2])
    for i in range(3):
        state_ref[i] = pack(places[i])
        state_ref[3 + i] = pack(others[i])
        for d in range(N_YZ):
            picks_ref[i, d] = others[i][d]
    for copy in names:
        copy.wait()
    for d in range(N_YZ):
        nball_ref[d * ATOMS : (d + 1) * ATOMS, :] = nbs[d]


def prepare(radial_ref, embed_ref, env_ref, latent_ref, read_ref, w1_ref, lt_ref, li_ref, bw_ref, ew_ref, rad_ref, rc_ref):
    radial = radial_ref[...].astype(F32)
    reads = read_ref[...].astype(F32).reshape(1, LATENT)
    stack = jnp.concatenate(
        [radial, embed_ref[1].astype(F32), embed_ref[0].astype(F32), jnp.zeros((104, LATENT), F32)], axis=0
    )
    w1_ref[...] = (stack.T * 0.5).astype(BF16)[:, 0:32]
    lt_ref[0:FEATURES, :] = env_ref[0].astype(F32).T.astype(BF16)
    for at in range(0, LATENT, 128):
        rows = latent_ref[0, at : at + 128, :].astype(F32)
        lt_ref[FEATURES : FEATURES + LATENT, at : at + 128] = (rows.T * 0.5).astype(BF16)
        bw_ref[FEATURES + at : FEATURES + at + 128, :] = (rows * (reads * 0.5)).astype(BF16)
    rows = latent_ref[0, LATENT : LATENT + FEATURES, :].astype(F32)
    li_ref[...] = (rows.T * 0.5).astype(BF16)
    bw_ref[0:FEATURES, :] = (rows * (reads * 0.5)).astype(BF16)
    column = jnp.broadcast_to(reads, (128, LATENT)).T
    ew_ref[:, 0:FEATURES] = env_ref[0]
    ew_ref[:, FEATURES : FEATURES + 16] = jnp.where(lanes_of((LATENT, 16)) == 0, column[:, 0:16], 0.0).astype(BF16)
    rad_ref[0:8, :] = (radial * 0.5).astype(BF16)
    rad_ref[8:16, :] = jnp.zeros((8, LATENT), BF16)
    rc_ref[...] = column


def middle_kernel(
    f_ref, state_ref, picks_ref, *rest
):
    refs, (next_ext_ref, half_two_ref, next_ref), scratch = rest[:9], rest[9:12], rest[12:]
    fsum, own, message, slab_in, up_in, down_in, up2_in, down2_in, sems = scratch
    me = lax.axis_index("yz")
    row = rows_of((8, 128))
    lane = lanes_of((8, 128))
    slab, above, below, above2, below2 = wide_partners()
    barrier = pltpu.get_barrier_semaphore()
    for _, g, q in slab + above + below + above2 + below2:
        pl.semaphore_signal(barrier, inc=1, device_id=(g, q), device_id_type=MESH)
    sure_forces(fsum, own, f_ref, refs)
    found = [[], [], []]
    for d, (tile0, tile1) in enumerate(fold(fsum)):
        tile0 = jnp.where(lane < NEAR, tile0, 0.0)
        ours, theirs = jnp.where(lane < 36, tile1, 0.0), jnp.where((lane >= 36) & (lane < 72), tile1, 0.0)
        found[0].append(dense(theirs, picks_ref[0, d, 5:6, :]))
        found[1].append(dense(tile0, picks_ref[1, d, 4:5, :]))
        found[2].append(dense(ours, picks_ref[2, d, 5:6, :]))
    for i in range(3):
        first = jnp.concatenate(found[i][0:2], axis=1)
        second = jnp.concatenate(found[i][2:4], axis=1)
        message[i] = jnp.where(row < 4, first, pltpu.roll(second, 4, 0))
    slab_in[me] = message[...]
    pl.semaphore_wait(barrier, 5 * N_YZ - 1)
    copies = []
    at = 0
    for group, part, buffer in (
        (above2, message.at[2:3], down2_in), (below2, message.at[0:1], up2_in), (above, message.at[1:3], down_in),
        (below, message.at[0:2], up_in), (slab, message, slab_in),
    ):
        for _, g, q in group:
            copies.append(send(part, buffer.at[me], sems, at, g, q))
            at += 1
    factors = []
    for i in range(3):
        place = state_ref[i]
        factors.append(0.5 * STEP * inverse_mass(jnp.where(row < 4, place[3:4], place[7:8])))
    for copy in copies:
        copy.wait()

    def over(pick):
        return (pick(0) + pick(1)) + (pick(2) + pick(3))

    forces = [
        over(lambda q: slab_in[q, 0]) + over(lambda q: down_in[q, 0]) + over(lambda q: down2_in[q, 0]),
        over(lambda q: slab_in[q, 1]) + over(lambda q: up_in[q, 0]) + over(lambda q: down_in[q, 1]),
        over(lambda q: slab_in[q, 2]) + over(lambda q: up_in[q, 1]) + over(lambda q: up2_in[q, 0]),
    ]
    coordinate = (row != 3) & (row != 7)
    places = []
    for i in range(3):
        place = state_ref[i]
        kick = factors[i] * forces[i]
        half_two = (state_ref[3 + i] + kick) + kick
        place = jnp.where(coordinate, place + STEP * half_two, place)
        tiles = [jnp.where(row == 4, picks_ref[i, d, 6:7, :], unpack(place, d)) for d in range(N_YZ)]
        places.append(tiles)
        if i == 1:
            own_half, own_place = unpack(half_two, 0), tiles[0]
            for d in range(1, N_YZ):
                own_half = jnp.where(me == d, unpack(half_two, d), own_half)
                own_place = jnp.where(me == d, tiles[d], own_place)
            half_two_ref[...] = own_half
            next_ref[...] = own_place
    picks = [[picks_ref[i, d] for d in range(N_YZ)] for i in range(3)]
    lists_from(next_ext_ref, places[1], picks[1], places[0], picks[0], places[2], picks[2])


def last_kernel(f_ref, *rest):
    refs, total_ref, scratch = rest[:9], rest[9], rest[10:]
    fsum, own, back0, back1, near, low, high, sems = scratch
    me = lax.axis_index("yz")
    greet()
    sure_forces(fsum, own, f_ref, refs)
    for d, (tile0, tile1) in enumerate(fold(fsum)):
        back0[d] = tile0
        back1[d] = tile1
    near[me] = back0[me]
    greeted()
    for copy in spread(lambda q: (back0.at[q], back1.at[q]), near, low, high, sems):
        copy.wait()
    total_ref[0], total_ref[1] = gathered(near, low, high)


def end_kernel(total_ref, half_ref, source_ref, pick_ref, pos_ref, vel_ref, force_ref):
    forces = own_forces(total_ref[0], total_ref[1], pick_ref)
    kick = 0.5 * STEP * inverse_mass(jnp.broadcast_to(source_ref[3:4, :], (8, 128))) * forces
    pos_ref[...] = source_ref[0:3, 0:ATOMS]
    vel_ref[...] = (half_ref[...] + kick)[0:3, 0:ATOMS]
    force_ref[...] = forces[0:3, 0:ATOMS]


def chain(items, add, ext_ref, nb_ref, w1_ref, lt_ref, li_ref, bw_ref, ew_ref, rad_ref, rc_ref):
    kind = rows_of((8, 128)).astype(F32)
    mid = (kind + 0.5) * 0.125
    geo, inputs = [], []
    for domain, slot, active in items:
        names = nb_ref[pl.ds(domain * ATOMS + slot, 1), :]
        valid = (names >= 0) & active
        names = jnp.maximum(names, 0)
        here = names < NEAR
        place = jnp.where(here, names, names - NEAR)
        tile0 = ext_ref[domain, :, 0:128]
        neigh = jnp.where(here, gather(tile0, place), gather(ext_ref[domain, :, 128:256], place))
        centre = gather(tile0, jnp.full((1, 128), slot, I32))
        u = (neigh - centre) * (1.0 / 6.0)
        sq = u[0:1] * u[0:1] + u[1:2] * u[1:2] + u[2:3] * u[2:3]
        inside = jnp.where(valid, jnp.maximum(1.0 - sq, 0.0), 0.0)
        env = inside * inside
        delta = sq - mid
        basis = jnp.exp(-128.0 * delta * delta)
        theirs = jnp.where(kind == neigh[3:4], 1.0, 0.0)
        own = jnp.where(kind == centre[3:4], 1.0, 0.0)
        inputs.append(jnp.concatenate([basis, theirs, own, jnp.zeros((8, 128), F32)], axis=0).astype(BF16))
        geo.append((names, u, inside, env, basis * delta))
    hp = mm(w1_ref[...], jnp.concatenate(inputs, axis=1)).astype(BF16)
    yield
    y1 = 1.0 + jnp.tanh(hp)
    h0 = hp * y1
    d1 = y1 + h0 * (2.0 - y1)
    yield
    zv = mm(lt_ref[...], h0)
    yield
    inner, kept = [], []
    for c, (names, u, inside, env, slope) in enumerate(geo):
        z = zv[0:FEATURES, c * 128 : c * 128 + 128]
        ue = [u[k : k + 1] * env for k in range(3)]
        c4 = [jnp.sum(z * ue[k], axis=1, keepdims=True) * SCALE for k in range(3)]
        q = c4[0] * ue[0] + c4[1] * ue[1] + c4[2] * ue[2]
        inner.append((z * q).astype(BF16))
        kept.append((z, ue, c4, q))
    yield
    vp = (zv[FEATURES:] + mm(li_ref[...], jnp.concatenate(inner, axis=1))).astype(BF16)
    yield
    y2 = 1.0 + jnp.tanh(vp)
    s2 = vp * y2
    d2 = y2 + s2 * (2.0 - y2)
    h2 = (h0 + s2).astype(F32)
    p = [jnp.sum(h2[:, c * 128 : c * 128 + 128] * rc_ref[...], axis=0, keepdims=True) for c in range(len(geo))]
    yield
    dj = mm(bw_ref[...], d2)
    yield
    sums, dws = [], []
    for c, (names, u, inside, env, slope) in enumerate(geo):
        z, ue, c4, q = kept[c]
        di = dj[0:FEATURES, c * 128 : c * 128 + 128]
        y = di * z
        g = [jnp.sum(y * (ue[k] * env), axis=1, keepdims=True) * SCALE for k in range(3)]
        dws.append(di * q + g[0] * u[0:1] + g[1] * u[1:2] + g[2] * u[2:3])
        ye = y * env
        sums.append([jnp.sum(c4[k] * ye + g[k] * z, axis=0, keepdims=True) for k in range(3)])
    dw = jnp.concatenate(dws, axis=1)
    ones = jnp.ones((8, dw.shape[1]), F32)
    dw = jnp.concatenate([dw, ones, jnp.zeros_like(ones)], axis=0).astype(BF16)
    yield
    a = dj[FEATURES:] + mm(ew_ref[...], dw)
    yield
    db = mm(rad_ref[...], a.astype(BF16) * d1)
    yield
    for c, (names, u, inside, env, slope) in enumerate(geo):
        domain, slot, active = items[c]
        lanes = slice(c * 128, c * 128 + 128)
        s = sums[c]
        dsq = env * jnp.sum(db[0:8, lanes] * slope, axis=0, keepdims=True) * -256.0
        denv = p[c] + u[0:1] * s[0] + u[1:2] * s[1] + u[2:3] * s[2]
        twice = 2.0 * (dsq - 2.0 * inside * denv)
        rows = [(env * s[k] + u[k : k + 1] * twice) * (1.0 / 6.0) for k in range(3)]
        du = jnp.concatenate(rows + [jnp.zeros((5, 128), F32)], axis=0)
        hi = du.astype(BF16)
        parts = jnp.concatenate([hi.astype(F32), du - hi.astype(F32)], axis=0).astype(BF16)
        pick = jnp.where(rows_of((EXT, 128)) == names, 1.0, 0.0).astype(BF16)
        out = lax.dot_general(parts, pick, NT, preferred_element_type=F32)
        out = out[0:8] + out[8:16]
        total = jnp.sum(du, axis=1, keepdims=True)
        add(domain, jnp.where(lanes_of((8, EXT)) == slot, total, 0.0) - out)
    yield


def drive(chains):
    while chains:
        chains = [one for one in chains if next(one, chains) is not chains]


def split(tile0, tail):
    lane = lanes_of((8, 128))
    far = jnp.where(lane < 128 - NEAR, pltpu.roll(tile0, 128 - NEAR, 1), pltpu.roll(tail, 128 - NEAR, 1))
    return jnp.where(lane < NEAR, tile0, 0.0), jnp.where(lane < NEAR, far, 0.0)


def pair_kernel(ext_ref, nb_ref, w1_ref, lt_ref, li_ref, bw_ref, ew_ref, rad_ref, rc_ref, f_ref, sums):
    refs = (ext_ref, nb_ref, w1_ref, lt_ref, li_ref, bw_ref, ew_ref, rad_ref, rc_ref)
    sums[...] = jnp.zeros_like(sums)
    ends = []
    total = jnp.int32(0)
    for d in range(N_YZ):
        total = total + lax.max(jnp.max(ext_ref[d, 4:5, 0:1]).astype(I32) - SURE, 0)
        ends.append(total)
    me = lax.axis_index("yz")
    first = (total * me) // N_YZ
    last = (total * (me + 1)) // N_YZ
    count = last - first
    step_size = 2 * CHAINS
    steps = lax.max(count - 2 * LAST + step_size - 1, 0) // step_size

    def add(domain, value):
        sums[domain, :, 0:EXT] += value

    def work(start, chains):
        made = []
        for g in range(chains):
            items = []
            for c in range(2):
                at = start + 2 * g + c
                active = at < last
                at = jnp.minimum(at, total - 1)
                domain = sum((at >= e).astype(I32) for e in ends[:-1])
                base = jnp.where(at >= ends[0], ends[0], 0)
                for e in ends[1:-1]:
                    base = jnp.where(at >= e, e, base)
                items.append((domain, at - base + SURE, active))
            made.append(chain(items, add, *refs))
        drive(made)

    def step(b, carry):
        work(first + b * 2 * CHAINS, CHAINS)
        return carry

    lax.fori_loop(0, steps, step, 0)
    start = first + steps * step_size

    @pl.when(start < last)
    def _():
        work(start, LAST)

    for d in range(N_YZ):
        f_ref[d, :, 0:128], f_ref[d, :, 128:256] = split(sums[d, :, 0:128], sums[d, :, 128:256])


def sure_forces(fsum, own, f_ref, refs):
    me = lax.axis_index("yz")
    values = []
    chains = []
    for g in range(SURE // 2):
        items = [(me, 2 * g + c, True) for c in range(2)]
        chains.append(chain(items, lambda domain, value: values.append(value), *refs))
    drive(chains)
    own[...] = jnp.zeros_like(own)
    own[:, 0:EXT] = functools.reduce(jnp.add, values)
    fsum[...] = f_ref[...]
    tile0, tile1 = split(own[:, 0:128], own[:, 128:256])
    fsum[me, :, 0:128] += tile0
    fsum[me, :, 128:256] += tile1


def body(
    positions, velocities, forces_start, species, live_atoms, send_list, neighbours, neighbour_count,
    radial_weight, species_embed, env_weight, latent_weight, readout,
):
    vm = pl.BlockSpec(memory_space=pltpu.VMEM)
    tile = jax.ShapeDtypeStruct((8, 128), F32)
    lists = jax.ShapeDtypeStruct((N_YZ, 8, 256), F32)
    atoms = jax.ShapeDtypeStruct((3, ATOMS), F32)
    four = pltpu.VMEM((N_YZ, 8, 128), F32)
    sums = pltpu.VMEM((N_YZ, 8, 256), F32)
    copies = pltpu.SemaphoreType.DMA((2, 3 * N_YZ - 1))
    params = functools.partial(pltpu.CompilerParams, vmem_limit_bytes=48 << 20)

    args = (
        positions, velocities, forces_start, species.reshape(1, -1), live_atoms.reshape(1, 1), send_list, neighbours,
        neighbour_count.reshape(1, -1), radial_weight, species_embed, env_weight, latent_weight,
        readout,
    )
    weights = [(LATENT, 32), (FEATURES + LATENT, LATENT), (LATENT, FEATURES), (FEATURES + LATENT, LATENT), (LATENT, FEATURES + 16), (16, LATENT)]
    out_shape = [lists, jax.ShapeDtypeStruct((N_YZ * ATOMS, SLOTS), I32), jax.ShapeDtypeStruct((6, 8, 128), F32)]
    out_shape += [jax.ShapeDtypeStruct((3, N_YZ, 8, 128), F32), jax.ShapeDtypeStruct((8, 128), I32)]
    out_shape += [jax.ShapeDtypeStruct(s, BF16) for s in weights] + [jax.ShapeDtypeStruct((LATENT, 128), F32)]
    scratch = [
        pltpu.VMEM((4, 8, 128), F32), pltpu.VMEM((8, 128), I32), pltpu.VMEM((2, 8, 128), F32), *[pltpu.VMEM((N_YZ, 2, 8, 128), F32)] * 3,
        pltpu.VMEM((N_YZ, ATOMS, SLOTS), I32), copies, pltpu.SemaphoreType.DMA((2, N_YZ - 1)),
        pltpu.VMEM(latent_weight.shape, BF16), pltpu.SemaphoreType.DMA,
    ]

    def first(*refs):
        first_kernel(refs[: len(args)], *refs[len(args) :])

    ext, names, state, picks, pick, *prepared = pl.pallas_call(
        first,
        out_shape=out_shape,
        in_specs=[vm] * 11 + [pl.BlockSpec(memory_space=pl.ANY), vm],
        out_specs=[vm] * len(out_shape),
        scratch_shapes=scratch,
        compiler_params=pltpu.CompilerParams(vmem_limit_bytes=103 << 19, collective_id=0, has_side_effects=True),
    )(*args)

    def forces_of(ext):
        return pl.pallas_call(
            pair_kernel,
            out_shape=lists,
            in_specs=[vm] * 9,
            out_specs=vm,
            scratch_shapes=[sums],
            compiler_params=params(),
        )(ext, names, *prepared)

    returning = [sums, pltpu.VMEM((8, 256), F32)] + [four] * 5 + [copies]
    next_ext, half, source = pl.pallas_call(
        middle_kernel,
        out_shape=[lists, tile, tile],
        in_specs=[vm] * 12,
        out_specs=[vm] * 3,
        scratch_shapes=[sums, pltpu.VMEM((8, 256), F32), pltpu.VMEM((3, 8, 128), F32)]
        + [pltpu.VMEM((N_YZ, n, 8, 128), F32) for n in (3, 2, 2, 1, 1)]
        + [pltpu.SemaphoreType.DMA((2, 5 * N_YZ - 1))],
        compiler_params=params(collective_id=1, has_side_effects=True),
    )(forces_of(ext), state, picks, ext, names, *prepared)

    totals = pl.pallas_call(
        last_kernel,
        out_shape=jax.ShapeDtypeStruct((2, 8, 128), F32),
        in_specs=[vm] * 10,
        out_specs=vm,
        scratch_shapes=returning,
        compiler_params=params(collective_id=2, has_side_effects=True),
    )(forces_of(next_ext), next_ext, names, *prepared)

    return pl.pallas_call(
        end_kernel,
        out_shape=[atoms] * 3,
        in_specs=[vm] * 4,
        out_specs=[vm] * 3,
        compiler_params=params(),
    )(totals, half, source, pick)


def solution(mesh):
    both = ("gx", "yz")
    atom = P(None, both)
    return jax.shard_map(
        body,
        mesh=mesh,
        in_specs=(atom, atom, atom, P(both), P(both), atom, P(both, None), P(both), P(), P(), P(), P(), P()),
        out_specs=(atom, atom, atom),
        check_vma=False,
    )
```

```python
import functools

import jax
import jax.numpy as jnp
from jax import lax
from jax.experimental import pallas as pl
from jax.experimental.pallas import tpu as pltpu
from jax.sharding import PartitionSpec as P

F32, BF16, I32 = jnp.float32, jnp.bfloat16, jnp.int32
MESH = pl.DeviceIdType.MESH
NT = (((1,), (1,)), ((), ()))

STEP = 0.25
MASSES = (1.008, 12.011, 14.007, 15.999, 32.06, 22.99, 35.45, 30.97)
ATOMS = 48
SLOTS = 128
GHOSTS = 12
N_YZ = 4
EXT = ATOMS + 8 * GHOSTS
NEAR = ATOMS + 2 * GHOSTS
LATENT = 512
FEATURES = 64
SCALE = 4.0 / SLOTS**0.5
CHAINS = 6
LAST = 3
SURE = 12


def mm(a, b):
    return jnp.dot(a, b, preferred_element_type=F32)


def lanes_of(shape):
    return lax.broadcasted_iota(I32, shape, len(shape) - 1)


def rows_of(shape):
    return lax.broadcasted_iota(I32, shape, 0)


def gather(table, idx):
    return jnp.take_along_axis(table, jnp.broadcast_to(idx, table.shape), axis=1)


def inverse_mass(species):
    total = jnp.zeros(species.shape, F32)
    for kind, mass in enumerate(MASSES):
        total = total + jnp.where(species == kind, jnp.float32(1.0 / mass), jnp.float32(0.0))
    return total


def partners():
    g, q, n = lax.axis_index("gx"), lax.axis_index("yz"), lax.axis_size("gx")
    slab = [(s, g, lax.rem(q + s, N_YZ)) for s in range(1, N_YZ)]
    up, down = lax.rem(g + 1, n), lax.rem(g + n - 1, n)
    above = [(s, up, lax.rem(q + s, N_YZ)) for s in range(N_YZ)]
    below = [(s, down, lax.rem(q + s, N_YZ)) for s in range(N_YZ)]
    return slab, above, below


def greet():
    slab, above, below = partners()
    barrier = pltpu.get_barrier_semaphore()
    for _, g, q in slab + above + below:
        pl.semaphore_signal(barrier, inc=1, device_id=(g, q), device_id_type=MESH)


def greeted():
    pl.semaphore_wait(pltpu.get_barrier_semaphore(), 3 * N_YZ - 1)


def wide_partners():
    g, q, n = lax.axis_index("gx"), lax.axis_index("yz"), lax.axis_size("gx")
    column = [lax.rem(q + s, N_YZ) for s in range(N_YZ)]
    return [[(s, lax.rem(g + n + step, n), column[s]) for s in range(step == 0, N_YZ)] for step in (0, 1, -1, 2, -2)]


def send(src, dst, sems, at, g, q):
    copy = pltpu.make_async_remote_copy(
        src_ref=src,
        dst_ref=dst,
        send_sem=sems.at[0, at],
        recv_sem=sems.at[1, at],
        device_id=(g, q),
        device_id_type=MESH,
    )
    copy.start()
    return copy


def spread(tiles, near, low, high, sems):
    me = lax.axis_index("yz")
    slab, above, below = partners()
    copies = []
    for s, g, q in slab:
        copies.append(send(tiles(q)[0], near.at[me], sems, s - 1, g, q))
    for s, g, q in above:
        copies.append(send(tiles(q)[1], low.at[me], sems, 3 + s, g, q))
    for s, g, q in below:
        copies.append(send(tiles(q)[1], high.at[me], sems, 7 + s, g, q))
    return copies


def assemble(ext_ref, near, low, high):
    lane = lanes_of((8, 128))
    for d in range(N_YZ):
        up, down = (d + 1) % N_YZ, (d - 1) % N_YZ
        ext_ref[d, :, 0:128] = jnp.where(
            lane < ATOMS, near[d], jnp.where(lane < ATOMS + GHOSTS, near[up], near[down])
        )
        hi = jnp.where(lane < 12, high[up], jnp.where(lane < 24, high[d], high[down]))
        lo = jnp.where(lane < 48, low[up], jnp.where(lane < 60, low[d], low[down]))
        ext_ref[d, :, 128:256] = jnp.where(lane < 36, hi, jnp.where(lane < 72, lo, 0.0))


def fold(f_ref):
    lane = lanes_of((8, 128))
    first = (lane < 12) | ((lane >= 36) & (lane < 48))
    second = (lane < 24) | ((lane >= 48) & (lane < 60))
    tiles = []
    for d in range(N_YZ):
        up, down = (d + 1) % N_YZ, (d - 1) % N_YZ
        tile0 = jnp.where(
            lane < ATOMS,
            f_ref[d, :, 0:128],
            jnp.where(lane < ATOMS + GHOSTS, f_ref[down, :, 0:128], f_ref[up, :, 0:128]),
        )
        tile1 = jnp.where(
            first,
            f_ref[down, :, 128:256],
            jnp.where(second, f_ref[d, :, 128:256], f_ref[up, :, 128:256]),
        )
        tiles.append((tile0, tile1))
    return tiles


def pack(tiles):
    low = jnp.where(lanes_of((8, 128)) < 64, tiles[0], pltpu.roll(tiles[1], 64, 1))
    high = jnp.where(lanes_of((8, 128)) < 64, tiles[2], pltpu.roll(tiles[3], 64, 1))
    return jnp.where(rows_of((8, 128)) < 4, low, pltpu.roll(high, 4, 0))


def unpack(tile, d):
    tile = pltpu.roll(tile, 64, 1) if d % 2 else tile
    return pltpu.roll(tile, 4, 0) if d >= 2 else tile


def dense(tile, picks):
    hi = tile.astype(BF16)
    parts = jnp.concatenate([hi.astype(F32), tile - hi.astype(F32)], axis=0).astype(BF16)
    hot = jnp.where(rows_of((64, 128)) == picks.astype(I32), 1.0, 0.0).astype(BF16)
    out = lax.dot_general(parts, hot, NT, preferred_element_type=F32)
    return out[0:8] + out[8:16]


def three(x):
    hi = x.astype(BF16)
    rest = x - hi.astype(F32)
    mid = rest.astype(BF16)
    low = rest - mid.astype(F32)
    return jnp.concatenate([hi.astype(F32), mid.astype(F32), low, jnp.zeros_like(x)], axis=0).astype(BF16)


def gathered(near, low, high):
    lane = lanes_of((8, 128))
    sum0 = (near[0] + near[1]) + (near[2] + near[3])
    lo = (low[0] + low[1]) + (low[2] + low[3])
    hi = (high[0] + high[1]) + (high[2] + high[3])
    sum0 = jnp.where(lane < NEAR, sum0, 0.0)
    return sum0, jnp.where(lane < 36, lo, jnp.where(lane < 72, hi, 0.0))


def own_forces(sum0, sum1, pick_ref):
    atom = rows_of((128, 128))
    pick0 = jnp.where(atom == pick_ref[0:1, :], 1.0, 0.0).astype(BF16)
    pick1 = jnp.where(atom == pick_ref[1:2, :], 1.0, 0.0).astype(BF16)
    parts = lax.dot_general(three(sum0), pick0, NT, preferred_element_type=F32)
    parts = parts + lax.dot_general(three(sum1), pick1, NT, preferred_element_type=F32)
    return (parts[0:8] + parts[8:16]) + parts[16:24]


def lists_from(ext_ref, near, near_picks, low, low_picks, high, high_picks):
    assemble(
        ext_ref,
        [gather(near[d], near_picks[d][4:5].astype(I32)) for d in range(N_YZ)],
        [gather(low[d], low_picks[d][5:6].astype(I32)) for d in range(N_YZ)],
        [gather(high[d], high_picks[d][5:6].astype(I32)) for d in range(N_YZ)],
    )


def first_kernel(
    in_refs,
    ext_ref, nball_ref, state_ref, picks_ref, pick_ref, w1_ref, lt_ref, li_ref, bw_ref, ew_ref, rad_ref, rc_ref,
    wide, sends, mine, near, low, high, nbs, sems, nbsems, latent, landed,
):
    greet()
    pos_ref, vel_ref, force_ref, spec_ref, live_ref, send_ref, nb_ref, count_ref = in_refs[:8]
    radial_ref, embed_ref, env_ref, latent_ref, read_ref = in_refs[8:]
    load = pltpu.make_async_copy(latent_ref, latent, landed)
    load.start()
    me = lax.axis_index("yz")
    slab, _, _ = partners()
    lane = lanes_of((8, 128))
    row = rows_of((8, 128))

    wide[...] = jnp.zeros_like(wide)
    wide[0, 0:3, 0:ATOMS] = pos_ref[...]
    wide[1, 0:3, 0:ATOMS] = vel_ref[...]
    wide[2, 0:3, 0:ATOMS] = force_ref[...]
    wide[3, 0:1, 0:ATOMS] = spec_ref[...].astype(F32)
    kinds = jnp.broadcast_to(wide[3, 0:1, :], (8, 128))
    half = wide[1] + 0.5 * STEP * inverse_mass(kinds) * wide[2]
    moved = wide[0] + STEP * half
    live = jnp.broadcast_to(live_ref[...].astype(F32), (8, 128))
    source = jnp.where(row < 3, moved, jnp.where(row == 3, kinds, live))

    sends[...] = jnp.zeros_like(sends)
    sends[:, 0:GHOSTS] = send_ref[...]
    pick0 = jnp.where(lane < ATOMS, lane, 127)
    pick1 = jnp.full((8, 128), 127, I32)
    for block, tile, at in ((3, 0, 48), (4, 0, 60), (0, 1, 0), (1, 1, 12), (2, 1, 24), (5, 1, 36), (6, 1, 48), (7, 1, 60)):
        names = jnp.broadcast_to(sends[block : block + 1, :], (8, 128))
        names = pltpu.roll(names, at, 1) if at else names
        here = (lane >= at) & (lane < at + GHOSTS)
        if tile == 0:
            pick0 = jnp.where(here, names, pick0)
        else:
            pick1 = jnp.where(here, names, pick1)
    pick_ref[...] = jnp.where(row == 0, pick0, pick1)
    mine[0] = source
    mine[1] = jnp.where(row < 3, half, jnp.where(row == 4, pick0.astype(F32), jnp.where(row == 5, pick1.astype(F32), live)))
    near[me] = mine[...]

    diagonal = rows_of((ATOMS, ATOMS)) == lanes_of((ATOMS, ATOMS))
    counts = jnp.sum(jnp.where(diagonal, count_ref[...].astype(F32), 0.0), axis=1, keepdims=True)
    names = nb_ref[...]
    shape = names.shape
    inner = (names >= 84) & (names < 108)
    outer = (names >= ATOMS) & (names < 84)
    names = jnp.where(inner, names - 36, jnp.where(outer, names + 24, names))
    used = (lanes_of(shape).astype(F32) < counts) & (
        rows_of(shape).astype(F32) < jnp.broadcast_to(live_ref[...].astype(F32), shape)
    )
    nbs[me] = jnp.where(used, names, -1)

    greeted()
    copies = spread(lambda q: (mine, mine), near, low, high, sems)
    names = [send(nbs.at[me], nbs.at[me], nbsems, s - 1, g, q) for s, g, q in slab]

    load.wait()
    prepare(radial_ref, embed_ref, env_ref, latent, read_ref, w1_ref, lt_ref, li_ref, bw_ref, ew_ref, rad_ref, rc_ref)

    for copy in copies:
        copy.wait()
    slabs = [[(buffer[d, 0], buffer[d, 1]) for d in range(N_YZ)] for buffer in (low, near, high)]
    places = [[one[0] for one in slab] for slab in slabs]
    others = [[one[1] for one in slab] for slab in slabs]
    lists_from(ext_ref, places[1], others[1], places[0], others[0], places[2], others[2])
    for i in range(3):
        state_ref[i] = pack(places[i])
        state_ref[3 + i] = pack(others[i])
        for d in range(N_YZ):
            picks_ref[i, d] = others[i][d]
    for copy in names:
        copy.wait()
    for d in range(N_YZ):
        nball_ref[d * ATOMS : (d + 1) * ATOMS, :] = nbs[d]


def prepare(radial_ref, embed_ref, env_ref, latent_ref, read_ref, w1_ref, lt_ref, li_ref, bw_ref, ew_ref, rad_ref, rc_ref):
    radial = radial_ref[...].astype(F32)
    reads = read_ref[...].astype(F32).reshape(1, LATENT)
    stack = jnp.concatenate(
        [radial, embed_ref[1].astype(F32), embed_ref[0].astype(F32), jnp.zeros((104, LATENT), F32)], axis=0
    )
    w1_ref[...] = (stack.T * 0.5).astype(BF16)[:, 0:32]
    lt_ref[0:FEATURES, :] = env_ref[0].astype(F32).T.astype(BF16)
    for at in range(0, LATENT, 128):
        rows = latent_ref[0, at : at + 128, :].astype(F32)
        lt_ref[FEATURES : FEATURES + LATENT, at : at + 128] = (rows.T * 0.5).astype(BF16)
        bw_ref[FEATURES + at : FEATURES + at + 128, :] = (rows * (reads * 0.5)).astype(BF16)
    rows = latent_ref[0, LATENT : LATENT + FEATURES, :].astype(F32)
    li_ref[...] = (rows.T * 0.5).astype(BF16)
    bw_ref[0:FEATURES, :] = (rows * (reads * 0.5)).astype(BF16)
    column = jnp.broadcast_to(reads, (128, LATENT)).T
    ew_ref[:, 0:FEATURES] = env_ref[0]
    ew_ref[:, FEATURES : FEATURES + 16] = jnp.where(lanes_of((LATENT, 16)) == 0, column[:, 0:16], 0.0).astype(BF16)
    rad_ref[0:8, :] = (radial * 0.5).astype(BF16)
    rad_ref[8:16, :] = jnp.zeros((8, LATENT), BF16)
    rc_ref[...] = column


def middle_kernel(
    f_ref, state_ref, picks_ref, *rest
):
    refs, (next_ext_ref, half_two_ref, next_ref), scratch = rest[:9], rest[9:12], rest[12:]
    fsum, own, message, slab_in, up_in, down_in, up2_in, down2_in, sems = scratch
    me = lax.axis_index("yz")
    row = rows_of((8, 128))
    lane = lanes_of((8, 128))
    slab, above, below, above2, below2 = wide_partners()
    barrier = pltpu.get_barrier_semaphore()
    for _, g, q in slab + above + below + above2 + below2:
        pl.semaphore_signal(barrier, inc=1, device_id=(g, q), device_id_type=MESH)
    sure_forces(fsum, own, f_ref, refs)
    found = [[], [], []]
    for d, (tile0, tile1) in enumerate(fold(fsum)):
        tile0 = jnp.where(lane < NEAR, tile0, 0.0)
        ours, theirs = jnp.where(lane < 36, tile1, 0.0), jnp.where((lane >= 36) & (lane < 72), tile1, 0.0)
        found[0].append(dense(theirs, picks_ref[0, d, 5:6, :]))
        found[1].append(dense(tile0, picks_ref[1, d, 4:5, :]))
        found[2].append(dense(ours, picks_ref[2, d, 5:6, :]))
    for i in range(3):
        first = jnp.concatenate(found[i][0:2], axis=1)
        second = jnp.concatenate(found[i][2:4], axis=1)
        message[i] = jnp.where(row < 4, first, pltpu.roll(second, 4, 0))
    slab_in[me] = message[...]
    pl.semaphore_wait(barrier, 5 * N_YZ - 1)
    copies = []
    at = 0
    for group, part, buffer in (
        (above2, message.at[2:3], down2_in), (below2, message.at[0:1], up2_in), (above, message.at[1:3], down_in),
        (below, message.at[0:2], up_in), (slab, message, slab_in),
    ):
        for _, g, q in group:
            copies.append(send(part, buffer.at[me], sems, at, g, q))
            at += 1
    factors = []
    for i in range(3):
        place = state_ref[i]
        factors.append(0.5 * STEP * inverse_mass(jnp.where(row < 4, place[3:4], place[7:8])))
    for copy in copies:
        copy.wait()

    def over(pick):
        return (pick(0) + pick(1)) + (pick(2) + pick(3))

    forces = [
        over(lambda q: slab_in[q, 0]) + over(lambda q: down_in[q, 0]) + over(lambda q: down2_in[q, 0]),
        over(lambda q: slab_in[q, 1]) + over(lambda q: up_in[q, 0]) + over(lambda q: down_in[q, 1]),
        over(lambda q: slab_in[q, 2]) + over(lambda q: up_in[q, 1]) + over(lambda q: up2_in[q, 0]),
    ]
    coordinate = (row != 3) & (row != 7)
    places = []
    for i in range(3):
        place = state_ref[i]
        kick = factors[i] * forces[i]
        half_two = (state_ref[3 + i] + kick) + kick
        place = jnp.where(coordinate, place + STEP * half_two, place)
        tiles = [jnp.where(row == 4, picks_ref[i, d, 6:7, :], unpack(place, d)) for d in range(N_YZ)]
        places.append(tiles)
        if i == 1:
            own_half, own_place = unpack(half_two, 0), tiles[0]
            for d in range(1, N_YZ):
                own_half = jnp.where(me == d, unpack(half_two, d), own_half)
                own_place = jnp.where(me == d, tiles[d], own_place)
            half_two_ref[...] = own_half
            next_ref[...] = own_place
    picks = [[picks_ref[i, d] for d in range(N_YZ)] for i in range(3)]
    lists_from(next_ext_ref, places[1], picks[1], places[0], picks[0], places[2], picks[2])


def last_kernel(f_ref, *rest):
    refs, total_ref, scratch = rest[:9], rest[9], rest[10:]
    fsum, own, back0, back1, near, low, high, sems = scratch
    me = lax.axis_index("yz")
    greet()
    sure_forces(fsum, own, f_ref, refs)
    for d, (tile0, tile1) in enumerate(fold(fsum)):
        back0[d] = tile0
        back1[d] = tile1
    near[me] = back0[me]
    greeted()
    for copy in spread(lambda q: (back0.at[q], back1.at[q]), near, low, high, sems):
        copy.wait()
    total_ref[0], total_ref[1] = gathered(near, low, high)


def end_kernel(total_ref, half_ref, source_ref, pick_ref, pos_ref, vel_ref, force_ref):
    forces = own_forces(total_ref[0], total_ref[1], pick_ref)
    kick = 0.5 * STEP * inverse_mass(jnp.broadcast_to(source_ref[3:4, :], (8, 128))) * forces
    pos_ref[...] = source_ref[0:3, 0:ATOMS]
    vel_ref[...] = (half_ref[...] + kick)[0:3, 0:ATOMS]
    force_ref[...] = forces[0:3, 0:ATOMS]


def chain(items, add, ext_ref, nb_ref, w1_ref, lt_ref, li_ref, bw_ref, ew_ref, rad_ref, rc_ref):
    kind = rows_of((8, 128)).astype(F32)
    mid = (kind + 0.5) * 0.125
    geo, inputs = [], []
    for domain, slot, active in items:
        names = nb_ref[pl.ds(domain * ATOMS + slot, 1), :]
        valid = (names >= 0) & active
        names = jnp.maximum(names, 0)
        here = names < NEAR
        place = jnp.where(here, names, names - NEAR)
        tile0 = ext_ref[domain, :, 0:128]
        neigh = jnp.where(here, gather(tile0, place), gather(ext_ref[domain, :, 128:256], place))
        centre = gather(tile0, jnp.full((1, 128), slot, I32))
        u = (neigh - centre) * (1.0 / 6.0)
        sq = u[0:1] * u[0:1] + u[1:2] * u[1:2] + u[2:3] * u[2:3]
        inside = jnp.where(valid, jnp.maximum(1.0 - sq, 0.0), 0.0)
        env = inside * inside
        delta = sq - mid
        basis = jnp.exp(-128.0 * delta * delta)
        theirs = jnp.where(kind == neigh[3:4], 1.0, 0.0)
        own = jnp.where(kind == centre[3:4], 1.0, 0.0)
        inputs.append(jnp.concatenate([basis, theirs, own, jnp.zeros((8, 128), F32)], axis=0).astype(BF16))
        geo.append((names, u, inside, env, basis * delta))
    hp = mm(w1_ref[...], jnp.concatenate(inputs, axis=1))
    yield
    y1 = 1.0 + jnp.tanh(hp)
    h0 = hp * y1
    d1 = y1 + h0 * (2.0 - y1)
    yield
    zv = mm(lt_ref[...], h0.astype(BF16))
    yield
    inner, kept = [], []
    for c, (names, u, inside, env, slope) in enumerate(geo):
        z = zv[0:FEATURES, c * 128 : c * 128 + 128]
        ue = [u[k : k + 1] * env for k in range(3)]
        c4 = [jnp.sum(z * ue[k], axis=1, keepdims=True) * SCALE for k in range(3)]
        q = c4[0] * ue[0] + c4[1] * ue[1] + c4[2] * ue[2]
        inner.append((z * q).astype(BF16))
        kept.append((z, ue, c4, q))
    yield
    vp = zv[FEATURES:] + mm(li_ref[...], jnp.concatenate(inner, axis=1))
    yield
    y2 = 1.0 + jnp.tanh(vp)
    s2 = vp * y2
    d2 = y2 + s2 * (2.0 - y2)
    h2 = h0 + s2
    p = [jnp.sum(h2[:, c * 128 : c * 128 + 128] * rc_ref[...], axis=0, keepdims=True) for c in range(len(geo))]
    yield
    dj = mm(bw_ref[...], d2.astype(BF16))
    yield
    sums, dws = [], []
    for c, (names, u, inside, env, slope) in enumerate(geo):
        z, ue, c4, q = kept[c]
        di = dj[0:FEATURES, c * 128 : c * 128 + 128]
        y = di * z
        g = [jnp.sum(y * (ue[k] * env), axis=1, keepdims=True) * SCALE for k in range(3)]
        dws.append(di * q + g[0] * u[0:1] + g[1] * u[1:2] + g[2] * u[2:3])
        ye = y * env
        sums.append([jnp.sum(c4[k] * ye + g[k] * z, axis=0, keepdims=True) for k in range(3)])
    dw = jnp.concatenate(dws, axis=1)
    ones = jnp.ones((8, dw.shape[1]), F32)
    dw = jnp.concatenate([dw, ones, jnp.zeros_like(ones)], axis=0).astype(BF16)
    yield
    a = dj[FEATURES:] + mm(ew_ref[...], dw)
    yield
    db = mm(rad_ref[...], (a * d1).astype(BF16))
    yield
    for c, (names, u, inside, env, slope) in enumerate(geo):
        domain, slot, active = items[c]
        lanes = slice(c * 128, c * 128 + 128)
        s = sums[c]
        dsq = env * jnp.sum(db[0:8, lanes] * slope, axis=0, keepdims=True) * -256.0
        denv = p[c] + u[0:1] * s[0] + u[1:2] * s[1] + u[2:3] * s[2]
        twice = 2.0 * (dsq - 2.0 * inside * denv)
        rows = [(env * s[k] + u[k : k + 1] * twice) * (1.0 / 6.0) for k in range(3)]
        du = jnp.concatenate(rows + [jnp.zeros((5, 128), F32)], axis=0)
        hi = du.astype(BF16)
        parts = jnp.concatenate([hi.astype(F32), du - hi.astype(F32)], axis=0).astype(BF16)
        pick = jnp.where(rows_of((EXT, 128)) == names, 1.0, 0.0).astype(BF16)
        out = lax.dot_general(parts, pick, NT, preferred_element_type=F32)
        out = out[0:8] + out[8:16]
        total = jnp.sum(du, axis=1, keepdims=True)
        add(domain, jnp.where(lanes_of((8, EXT)) == slot, total, 0.0) - out)
    yield


def drive(chains):
    while chains:
        chains = [one for one in chains if next(one, chains) is not chains]


def split(tile0, tail):
    lane = lanes_of((8, 128))
    far = jnp.where(lane < 128 - NEAR, pltpu.roll(tile0, 128 - NEAR, 1), pltpu.roll(tail, 128 - NEAR, 1))
    return jnp.where(lane < NEAR, tile0, 0.0), jnp.where(lane < NEAR, far, 0.0)


def pair_kernel(ext_ref, nb_ref, w1_ref, lt_ref, li_ref, bw_ref, ew_ref, rad_ref, rc_ref, f_ref, sums):
    refs = (ext_ref, nb_ref, w1_ref, lt_ref, li_ref, bw_ref, ew_ref, rad_ref, rc_ref)
    sums[...] = jnp.zeros_like(sums)
    ends = []
    total = jnp.int32(0)
    for d in range(N_YZ):
        total = total + lax.max(jnp.max(ext_ref[d, 4:5, 0:1]).astype(I32) - SURE, 0)
        ends.append(total)
    me = lax.axis_index("yz")
    first = (total * me) // N_YZ
    last = (total * (me + 1)) // N_YZ
    count = last - first
    step_size = 2 * CHAINS
    steps = lax.max(count - 2 * LAST + step_size - 1, 0) // step_size

    def add(domain, value):
        sums[domain, :, 0:EXT] += value

    def work(start, chains):
        made = []
        for g in range(chains):
            items = []
            for c in range(2):
                at = start + 2 * g + c
                active = at < last
                at = jnp.minimum(at, total - 1)
                domain = sum((at >= e).astype(I32) for e in ends[:-1])
                base = jnp.where(at >= ends[0], ends[0], 0)
                for e in ends[1:-1]:
                    base = jnp.where(at >= e, e, base)
                items.append((domain, at - base + SURE, active))
            made.append(chain(items, add, *refs))
        drive(made)

    def step(b, carry):
        work(first + b * 2 * CHAINS, CHAINS)
        return carry

    lax.fori_loop(0, steps, step, 0)
    start = first + steps * step_size

    @pl.when(start < last)
    def _():
        work(start, LAST)

    for d in range(N_YZ):
        f_ref[d, :, 0:128], f_ref[d, :, 128:256] = split(sums[d, :, 0:128], sums[d, :, 128:256])


def sure_forces(fsum, own, f_ref, refs):
    me = lax.axis_index("yz")
    values = []
    chains = []
    for g in range(SURE // 2):
        items = [(me, 2 * g + c, True) for c in range(2)]
        chains.append(chain(items, lambda domain, value: values.append(value), *refs))
    drive(chains)
    own[...] = jnp.zeros_like(own)
    own[:, 0:EXT] = functools.reduce(jnp.add, values)
    fsum[...] = f_ref[...]
    tile0, tile1 = split(own[:, 0:128], own[:, 128:256])
    fsum[me, :, 0:128] += tile0
    fsum[me, :, 128:256] += tile1


def body(
    positions, velocities, forces_start, species, live_atoms, send_list, neighbours, neighbour_count,
    radial_weight, species_embed, env_weight, latent_weight, readout,
):
    vm = pl.BlockSpec(memory_space=pltpu.VMEM)
    tile = jax.ShapeDtypeStruct((8, 128), F32)
    lists = jax.ShapeDtypeStruct((N_YZ, 8, 256), F32)
    atoms = jax.ShapeDtypeStruct((3, ATOMS), F32)
    four = pltpu.VMEM((N_YZ, 8, 128), F32)
    sums = pltpu.VMEM((N_YZ, 8, 256), F32)
    copies = pltpu.SemaphoreType.DMA((2, 3 * N_YZ - 1))
    params = functools.partial(pltpu.CompilerParams, vmem_limit_bytes=48 << 20)

    args = (
        positions, velocities, forces_start, species.reshape(1, -1), live_atoms.reshape(1, 1), send_list, neighbours,
        neighbour_count.reshape(1, -1), radial_weight, species_embed, env_weight, latent_weight,
        readout,
    )
    weights = [(LATENT, 32), (FEATURES + LATENT, LATENT), (LATENT, FEATURES), (FEATURES + LATENT, LATENT), (LATENT, FEATURES + 16), (16, LATENT)]
    out_shape = [lists, jax.ShapeDtypeStruct((N_YZ * ATOMS, SLOTS), I32), jax.ShapeDtypeStruct((6, 8, 128), F32)]
    out_shape += [jax.ShapeDtypeStruct((3, N_YZ, 8, 128), F32), jax.ShapeDtypeStruct((8, 128), I32)]
    out_shape += [jax.ShapeDtypeStruct(s, BF16) for s in weights] + [jax.ShapeDtypeStruct((LATENT, 128), F32)]
    scratch = [
        pltpu.VMEM((4, 8, 128), F32), pltpu.VMEM((8, 128), I32), pltpu.VMEM((2, 8, 128), F32), *[pltpu.VMEM((N_YZ, 2, 8, 128), F32)] * 3,
        pltpu.VMEM((N_YZ, ATOMS, SLOTS), I32), copies, pltpu.SemaphoreType.DMA((2, N_YZ - 1)),
        pltpu.VMEM(latent_weight.shape, BF16), pltpu.SemaphoreType.DMA,
    ]

    def first(*refs):
        first_kernel(refs[: len(args)], *refs[len(args) :])

    ext, names, state, picks, pick, *prepared = pl.pallas_call(
        first,
        out_shape=out_shape,
        in_specs=[vm] * 11 + [pl.BlockSpec(memory_space=pl.ANY), vm],
        out_specs=[vm] * len(out_shape),
        scratch_shapes=scratch,
        compiler_params=pltpu.CompilerParams(vmem_limit_bytes=103 << 19, collective_id=0, has_side_effects=True),
    )(*args)

    def forces_of(ext):
        return pl.pallas_call(
            pair_kernel,
            out_shape=lists,
            in_specs=[vm] * 9,
            out_specs=vm,
            scratch_shapes=[sums],
            compiler_params=params(),
        )(ext, names, *prepared)

    returning = [sums, pltpu.VMEM((8, 256), F32)] + [four] * 5 + [copies]
    next_ext, half, source = pl.pallas_call(
        middle_kernel,
        out_shape=[lists, tile, tile],
        in_specs=[vm] * 12,
        out_specs=[vm] * 3,
        scratch_shapes=[sums, pltpu.VMEM((8, 256), F32), pltpu.VMEM((3, 8, 128), F32)]
        + [pltpu.VMEM((N_YZ, n, 8, 128), F32) for n in (3, 2, 2, 1, 1)]
        + [pltpu.SemaphoreType.DMA((2, 5 * N_YZ - 1))],
        compiler_params=params(collective_id=1, has_side_effects=True),
    )(forces_of(ext), state, picks, ext, names, *prepared)

    totals = pl.pallas_call(
        last_kernel,
        out_shape=jax.ShapeDtypeStruct((2, 8, 128), F32),
        in_specs=[vm] * 10,
        out_specs=vm,
        scratch_shapes=returning,
        compiler_params=params(collective_id=2, has_side_effects=True),
    )(forces_of(next_ext), next_ext, names, *prepared)

    return pl.pallas_call(
        end_kernel,
        out_shape=[atoms] * 3,
        in_specs=[vm] * 4,
        out_specs=[vm] * 3,
        compiler_params=params(),
    )(totals, half, source, pick)


def solution(mesh):
    both = ("gx", "yz")
    atom = P(None, both)
    return jax.shard_map(
        body,
        mesh=mesh,
        in_specs=(atom, atom, atom, P(both), P(both), atom, P(both, None), P(both), P(), P(), P(), P(), P()),
        out_specs=(atom, atom, atom),
        check_vma=False,
    )
```
